512 devices in a mesh: gx: 64 (over z, y_hi, x), gy: 8 (over y_lo, core).
Axes of the slice: x: 4, y: 8 (y_hi: 2, y_lo: 4; y = y_hi * 4 + y_lo), z: 8, core: 2. Of those that a mesh axis runs over, the one named last changes fastest.
Arguments:
- features: bfloat16 [3584, 32, 5120], P('gx', None, 'gy'), may hold values from -6 to 6
- weight_x: int32 [3584], P('gx'), may hold values from 1 to 16
- weight_y: int32 [320], P('gy'), may hold values from 1 to 16
- conv_weight: bfloat16 [32, 32], replicated, may hold values from -1 to 1
- class_bias: float32 [32], replicated, may hold values from -4 to 4
Outputs:
- level0: bfloat16 [3072, 32, 4096], P('gx', None, 'gy')
- level1: bfloat16 [1536, 32, 1024], P('gx', None, 'gy')
- level2: bfloat16 [768, 32, 256], P('gx', None, 'gy')
- level3: bfloat16 [384, 32, 64], P('gx')
- level4: bfloat16 [192, 32, 16], P('gx')
The draws below stay inside these ranges and needn't reach their ends.
All inputs are finite; a program needn't handle non-finite values.
Results may differ from the reference program's by a relative error of at most 0.006.
Values may be sent and summed in bfloat16 or wider, within the bound.
A program may use at most 64 MiB of HBM per device.

```python
import jax
import jax.numpy as jnp
from jax import lax

CH = 32
CLS = 32
BX = 48
BY = 32
BZ = 16
MARGIN = 8
NY = 256
PX = 3584
PY = 320
N_GX = 64
N_GY = 8


def set_ends(array, key, smallest, high):
    longest = array.shape.index(max(array.shape))
    spots = []
    for shift in (0, 1):
        where = [jax.random.randint(jax.random.fold_in(key, axis), (), 0, length) for axis, length in enumerate(array.shape)]
        where[longest] = (where[longest] + shift) % array.shape[longest]
        spots.append(tuple(where))
    return array.at[spots[0]].set(smallest).at[spots[1]].set(high)


def shard_levels(key, shape, shards, least, high):
    gain = 1.0
    for position, blocks in shards:
        draws = jax.random.uniform(jax.random.fold_in(jax.random.fold_in(key, 6), position), (blocks,), jnp.float32, least / len(shards), high / len(shards))
        gain = gain * jnp.repeat(jnp.exp(draws), shape[position] // blocks).reshape((-1,) + (1,) * (len(shape) - 1 - position))
    return gain


def noise(stream_key, dims, scale, most, shards=(), kind=jnp.bfloat16):
    level = shard_levels(stream_key, dims, shards, -0.22, 0.18) if shards else 1.0
    array = jax.random.normal(stream_key, dims, jnp.float32) * scale * level
    return jnp.minimum(jnp.maximum(array, -most), most).astype(kind)


def setup_inputs(seed: int = 0) -> dict:
    arg_keys = jax.random.split(jax.random.key(seed), 6)
    features = noise(arg_keys[0], (PX, CH, PY * BZ), 1.0, 6.0, ((0, 64), (2, 8)))
    weight_x = set_ends(jax.random.randint(arg_keys[1], (PX,), 1, 17), jax.random.fold_in(arg_keys[1], 1), 1, 16).astype(jnp.int32)
    weight_y = set_ends(jax.random.randint(arg_keys[2], (PY,), 1, 17), jax.random.fold_in(arg_keys[2], 1), 1, 16).astype(jnp.int32)
    conv_weight = noise(arg_keys[3], (CH, CLS), CH ** -0.5, 1.0)
    class_bias = noise(arg_keys[4], (CLS,), 1.0, 4.0, (), jnp.float32)
    return dict(features=features, weight_x=weight_x, weight_y=weight_y, conv_weight=conv_weight, class_bias=class_bias)


def shrink(volume):
    xs, ks, ys, zs = volume.shape
    parts = volume.reshape(xs // 2, 2, ks, ys // 2, 2, zs // 2, 2).astype(jnp.float32)
    return jnp.mean(parts, axis=(1, 4, 6)).astype(jnp.bfloat16)


def flatten(volume):
    xs, ks, ys, zs = volume.shape
    return volume.reshape(xs, ks, ys * zs)


def reference(features, weight_x, weight_y, conv_weight, class_bias):
    xe = BX + MARGIN
    ye = BY + MARGIN
    patches = features.reshape(N_GX, xe, CH, N_GY, ye, BZ)
    wxs = weight_x.reshape(N_GX, xe).astype(jnp.float32)
    wys = weight_y.reshape(N_GY, ye).astype(jnp.float32)
    kernel = conv_weight.astype(jnp.float32)

    def patch_terms(index):
        feats = lax.dynamic_index_in_dim(patches, index, 0, keepdims=False).astype(jnp.float32)
        logit = jnp.einsum("xcgyz,ck->xkgyz", feats, kernel) + class_bias[None, :, None, None, None]
        logit = logit.astype(jnp.bfloat16).astype(jnp.float32)
        row_w = lax.dynamic_index_in_dim(wxs, index, 0, keepdims=False)
        weight = row_w[:, None, None] * wys[None, :, :]
        return logit * weight[:, None, :, :, None], weight

    def one_row(index):
        numer, denom = patch_terms(index)
        prev_n, prev_d = patch_terms(jnp.maximum(index - 1, 0))
        keep = (index > 0).astype(jnp.float32)
        numer = numer[:BX].at[:MARGIN].add(keep * prev_n[BX:])
        denom = denom[:BX].at[:MARGIN].add(keep * prev_d[BX:])
        margin_n = numer[:, :, :, BY:]
        moved_n = jnp.concatenate([jnp.zeros_like(margin_n[:, :, :1]), margin_n[:, :, :-1]], axis=2)
        numer = numer[:, :, :, :BY].at[:, :, :, :MARGIN].add(moved_n)
        margin_d = denom[:, :, BY:]
        moved_d = jnp.concatenate([jnp.zeros_like(margin_d[:, :1]), margin_d[:, :-1]], axis=1)
        denom = denom[:, :, :BY].at[:, :, :MARGIN].add(moved_d)
        blended = (numer / denom[:, None, :, :, None]).astype(jnp.bfloat16).reshape(BX, CLS, NY, BZ)
        first = shrink(blended)
        second = shrink(first)
        third = shrink(second)
        fourth = shrink(third)
        return flatten(blended), flatten(first), flatten(second), flatten(third), flatten(fourth)

    rows = lax.map(one_row, jnp.arange(N_GX, dtype=jnp.int32))
    results = []
    for level in rows:
        results.append(level.reshape(level.shape[0] * level.shape[1], level.shape[2], level.shape[3]))
    return results[0], results[1], results[2], results[3], results[4]
```

```python
import jax
import jax.numpy as jnp
from jax import lax
from jax.experimental import pallas as pl
from jax.experimental.pallas import tpu as pltpu
from jax.sharding import PartitionSpec as P

MESH = pl.DeviceIdType.MESH
F32 = jnp.float32
BF16 = jnp.bfloat16

CHUNKS = 6
ROWS = 256
PIECES = ((1, 0), (1, 1), (2, 0), (2, 1), (3, 0), (3, 1), (0, 0), (0, 1))
WAYS = (2, -2, 2, -2, -2, -2, 2, -2, 2)


def iota(shape, dim):
    return lax.broadcasted_iota(jnp.int32, shape, dim)


def one_hot(condition, value):
    return jnp.where(condition, value, 0.0).astype(BF16)


def dot(a, b):
    return jnp.dot(a, b, preferred_element_type=F32)


def device(x, y, z, core):
    return (z * 8 + (y // 4) * 4 + x, (y % 4) * 2 + core)


def kernel(
    features,
    weight_x,
    weight_y,
    conv,
    bias,
    level0,
    level1,
    level2,
    level3,
    level4,
    held,
    block,
    out0,
    out1,
    y_out,
    y_in,
    corner_out,
    corner_in,
    x_out,
    x_in,
    xw_out,
    xw_in,
    relay,
    relay_w,
    first_y,
    shares,
    pool1,
    pool2,
    pool3,
    pool4,
    own_third,
    all_third,
    load_sem,
    store_sem,
    y_send,
    y_recv,
    x_send,
    x_recv,
    hop_send,
    hop_recv,
    on_send,
    third_send,
    third_recv,
):
    gx = lax.axis_index("gx")
    gy = lax.axis_index("gy")
    x, z, core = gx % 4, gx // 8, gy % 2
    y = (gx // 4) % 2 * 4 + gy // 2
    near = x < 3
    far = jnp.logical_and(x == 3, gx < 63)
    has_left = gx > 0
    has_up = gy > 0
    has_down = gy < 7

    def carries(way):
        source = (y - way + 8) % 8
        last = jnp.logical_and(z == 7, source >= 4)
        return jnp.logical_and(x == 0, jnp.logical_not(last))

    def carry_to(way):
        source = (y - way + 8) % 8
        return device(0, (source + 4) % 8, z + source // 4, core)

    far_in = jnp.logical_and(x == 0, has_left)

    loads = [
        pltpu.make_async_copy(features.at[i], held.at[i], load_sem.at[i])
        for i in range(7)
    ]
    loads[6].start()
    for i in range(CHUNKS):
        loads[i].start()

    barrier = pltpu.get_barrier_semaphore()

    def greet(target):
        pl.semaphore_signal(barrier, inc=1, device_id=target, device_id_type=MESH)

    for way in (2, -2):

        @pl.when(carries(way))
        def _():
            greet(device(3, (y - way + 8) % 8, z, core))

        @pl.when(far_in)
        def _():
            before = z - jnp.where(y < 4, 1, 0)
            greet(device(0, (y + 4 + way) % 8, before, core))

    @pl.when(jnp.logical_and(has_left, x > 0))
    def _():
        greet((gx - 1, gy))

    for o in range(1, 8):
        greet((gx, (gy + o) % 8))

    pick = (iota((ROWS, 32), 0) % 32) == iota((ROWS, 32), 1)
    spread = one_hot(pick, 1.0)
    dims = (((1,), (1,)), ((), ()))
    tall = lax.dot_general(spread, conv[...], dims, preferred_element_type=F32)
    wide = lax.dot_general(
        tall.astype(BF16), spread, dims, preferred_element_type=F32
    )
    same = iota((ROWS, ROWS), 0) // 32 == iota((ROWS, ROWS), 1) // 32
    block[...] = jnp.where(same, wide, 0.0).astype(BF16)
    bias_column = jnp.sum(jnp.where(pick, bias[...], 0.0), axis=1, keepdims=True)

    def logits(i):
        return (dot(block[...], held[i]) + bias_column).astype(BF16)

    lane_y = iota((8, 128), 1) // 16
    row = iota((8, 128), 0)
    wy_own = jnp.zeros((8, 128), F32)
    wy_last = jnp.zeros((8, 128), F32)
    wx_own = jnp.zeros((8, 128), F32)
    wx_last = jnp.zeros((8, 128), F32)
    for k in range(8):
        wy_own = jnp.where(lane_y == k, weight_y[k].astype(F32), wy_own)
        wy_last = jnp.where(lane_y == k, weight_y[32 + k].astype(F32), wy_last)
        wx_own = jnp.where(row == k, weight_x[k].astype(F32), wx_own)
        wx_last = jnp.where(row == k, weight_x[48 + k].astype(F32), wx_last)
    corner_out[ROWS:, :] = jnp.concatenate([wy_last, wy_last], axis=0).astype(BF16)
    xw_out[...] = jnp.concatenate([wx_last, wx_last], axis=0).astype(BF16)

    loads[6].wait()
    margin = logits(6)
    corner_out[:ROWS, :] = margin[:, 512:]
    for t in range(4):
        x_out[t] = margin[:, 128 * t : 128 * (t + 1)]

    peers = 7 + near.astype(jnp.int32) + 2 * far.astype(jnp.int32)
    for way in (2, -2):
        peers = peers + carries(way).astype(jnp.int32)
    pl.semaphore_wait(barrier, peers)

    def remote(src, dst, send, recv, target):
        return pltpu.make_async_remote_copy(
            src_ref=src,
            dst_ref=dst,
            send_sem=send,
            recv_sem=recv,
            device_id=target,
            device_id_type=MESH,
        )

    down = (gx, (gy + 1) % 8)
    corner_copy = remote(corner_out, corner_in, y_send.at[6], y_recv.at[6], down)
    y_copies = [
        remote(y_out.at[i], y_in.at[i], y_send.at[i], y_recv.at[i], down)
        for i in range(CHUNKS)
    ]

    def part(ref, h):
        t, half = PIECES[h]
        return ref.at[t, pl.ds(128 * half, 128)]

    def direct(h):
        target = ((gx + 1) % 64, gy)
        src, dst = (xw_out, xw_in) if h == 8 else (part(x_out, h), part(x_in, h))
        return remote(src, dst, x_send.at[h], x_recv.at[h], target)

    def hop(h):
        target = device(0, (y + WAYS[h] + 8) % 8, z, core)
        src, dst = (xw_out, relay_w) if h == 8 else (part(x_out, h), relay.at[h])
        return remote(src, dst, hop_send.at[h], hop_recv.at[h], target)

    def onward(h):
        target = carry_to(WAYS[h])
        src, dst = (relay_w, xw_in) if h == 8 else (relay.at[h], part(x_in, h))
        return remote(src, dst, on_send.at[h], x_recv.at[h], target)

    def send_x(pieces):
        @pl.when(near)
        def _():
            for h in pieces:
                direct(h).start()

        @pl.when(far)
        def _():
            for h in pieces:
                hop(h).start()

    @pl.when(has_down)
    def _():
        corner_copy.start()

    send_x((8, 0, 1, 2, 3, 4, 5))

    for i in range(CHUNKS):
        loads[i].wait()
        value = logits(i)
        y_out[i] = value[:, 512:]
        out0[i] = value[:, :512]

        @pl.when(has_down)
        def _():
            y_copies[i].start()

        if i == 3:
            @pl.when(has_up)
            def _():
                corner_copy.wait_recv()
                wy_up = corner_in[ROWS:, :].astype(F32)[:8]
                total = wy_own + wy_up
                own_share, up_share = wy_own / total, wy_up / total
                shares[0] = own_share
                shares[1] = up_share
                x_out[0] = (
                    x_out[0].astype(F32) * own_share[:1]
                    + corner_in[:ROWS, :].astype(F32) * up_share[:1]
                ).astype(BF16)

            send_x((6, 7))

    source, target = iota((512, 128), 0), iota((512, 128), 1)
    pool1[...] = one_hot(source // 32 * 8 + source % 16 // 2 == target, 0.125)
    source, target = iota((128, 128), 0), iota((128, 128), 1)
    pool2[...] = one_hot(source // 16 * 4 + source % 8 // 2 == target, 0.125)
    pool3[...] = one_hot(
        jnp.logical_and(
            source // 8 * 2 + source % 4 // 2 + gy * 8 == target, source < 32
        ),
        0.125,
    )
    pool4[...] = one_hot(jnp.logical_and(source // 4 == target, source < 64), 0.125)

    for h in (8, 0, 1, 2, 3, 4, 5, 6, 7):

        @pl.when(carries(WAYS[h]))
        def _():
            hop(h).wait_recv()
            onward(h).start()

    third = jnp.zeros((16, 128), F32)

    def mips(i, third):
        pooled = dot(out0[i], pool1[...]).reshape(4, 2, 32, 128)
        first = (pooled[:, 0] + pooled[:, 1]).astype(BF16).reshape(128, 128)
        out1[i] = first
        pltpu.make_async_copy(out0.at[i], level0.at[i], store_sem.at[i]).start()
        pltpu.make_async_copy(out1.at[i], level1.at[i], store_sem.at[6 + i]).start()
        pooled = dot(first, pool2[...]).reshape(2, 2, 32, 128)
        second = (pooled[:, 0] + pooled[:, 1]).astype(BF16).reshape(64, 128)
        level2[pl.ds(64 * i, 64), :] = second[:, :32]
        pooled = dot(second, pool3[...])
        pooled = pooled[:32] + pooled[32:]
        third = third + pltpu.roll(pooled[:16], 8 * i, 1)
        return third + pltpu.roll(pooled[16:], 8 * (6 + i), 1)

    for i in range(1, CHUNKS):

        @pl.when(has_up)
        def _():
            y_copies[i].wait_recv()
            out0[i, :, :128] = (
                out0[i, :, :128].astype(F32) * shares[0, :1]
                + y_in[i].astype(F32) * shares[1, :1]
            ).astype(BF16)

        third = mips(i, third)

    first_y[...] = out0[0, :, :128].astype(F32)

    @pl.when(has_up)
    def _():
        y_copies[0].wait_recv()
        first_y[...] = first_y[...] * shares[0, :1] + y_in[0].astype(F32) * shares[1, :1]

    out0[0, :, :128] = first_y[...].astype(BF16)

    @pl.when(has_left)
    def _():
        for h in (8, 0, 1, 2, 3, 4, 5, 6, 7):
            direct(h).wait_recv()
        wx_left = xw_in[...].astype(F32)[:8]
        total = wx_own + wx_left
        own_share, left_share = wx_own / total, wx_left / total
        for a in range(8):
            rows = pl.ds(32 * a, 32)
            mine, theirs = own_share[a : a + 1], left_share[a : a + 1]
            for t in range(4):
                lanes = pl.ds(128 * t, 128)
                own = first_y[rows, :] if t == 0 else out0[0, rows, lanes].astype(F32)
                out0[0, rows, lanes] = (
                    own * mine + x_in[t, rows, :].astype(F32) * theirs
                ).astype(BF16)

    third = mips(0, third)

    own_third[...] = third.astype(BF16)
    third_copies = [
        remote(
            own_third,
            all_third.at[o],
            third_send.at[o],
            third_recv.at[o],
            (gx, (gy + o) % 8),
        )
        for o in range(1, 8)
    ]
    for copy in third_copies:
        copy.start()
    for copy in third_copies:
        copy.wait_recv()
    group = iota((16, 128), 1) // 8
    parts = [own_third[...].astype(F32)] + [
        all_third[o].astype(F32) for o in range(1, 8)
    ]
    rows = [None] * 12
    for q in range(12):
        owner = (group - q + 16) % 16
        value = jnp.zeros((16, 128), F32)
        for o in range(8):
            value = jnp.where(owner == (gy - o + 8) % 8, parts[o], value)
        half, i = q // 6, q % 6
        rows[2 * i + half] = pltpu.roll(value, (128 - 8 * q) % 128, 1)
    whole = jnp.concatenate(rows, axis=0).astype(BF16)
    level3[...] = whole[:, :64]
    pooled = dot(whole, pool4[...]).reshape(3, 2, 32, 128)
    fourth = (pooled[:, 0] + pooled[:, 1]).astype(BF16).reshape(96, 128)
    level4[...] = fourth[:, :16]

    for copy in third_copies:
        copy.wait_send()

    @pl.when(has_down)
    def _():
        corner_copy.wait_send()
        for i in range(CHUNKS):
            y_copies[i].wait_send()

    @pl.when(near)
    def _():
        for h in range(9):
            direct(h).wait_send()

    @pl.when(far)
    def _():
        for h in range(9):
            hop(h).wait_send()

    for h in range(9):

        @pl.when(carries(WAYS[h]))
        def _():
            onward(h).wait_send()

    for i in range(CHUNKS):
        pltpu.make_async_copy(out0.at[i], level0.at[i], store_sem.at[i]).wait()
        pltpu.make_async_copy(out1.at[i], level1.at[i], store_sem.at[6 + i]).wait()


def shards(features, weight_x, weight_y, conv_weight, class_bias):
    vmem = pl.BlockSpec(memory_space=pltpu.VMEM)
    smem = pl.BlockSpec(memory_space=pltpu.SMEM)
    hbm = pl.BlockSpec(memory_space=pl.ANY)
    dma = pltpu.SemaphoreType.DMA
    outs = pl.pallas_call(
        kernel,
        name="blend",
        out_shape=(
            jax.ShapeDtypeStruct((6, 256, 512), BF16),
            jax.ShapeDtypeStruct((6, 128, 128), BF16),
            jax.ShapeDtypeStruct((384, 32), BF16),
            jax.ShapeDtypeStruct((192, 64), BF16),
            jax.ShapeDtypeStruct((96, 16), BF16),
        ),
        in_specs=[hbm, smem, smem, vmem, vmem],
        out_specs=(hbm, hbm, vmem, vmem, vmem),
        scratch_shapes=[
            pltpu.VMEM((7, 256, 640), BF16),
            pltpu.VMEM((256, 256), BF16),
            pltpu.VMEM((6, 256, 512), BF16),
            pltpu.VMEM((6, 128, 128), BF16),
            pltpu.VMEM((6, 256, 128), BF16),
            pltpu.VMEM((6, 256, 128), BF16),
            pltpu.VMEM((272, 128), BF16),
            pltpu.VMEM((272, 128), BF16),
            pltpu.VMEM((4, 256, 128), BF16),
            pltpu.VMEM((4, 256, 128), BF16),
            pltpu.VMEM((16, 128), BF16),
            pltpu.VMEM((16, 128), BF16),
            pltpu.VMEM((8, 128, 128), BF16),
            pltpu.VMEM((16, 128), BF16),
            pltpu.VMEM((256, 128), F32),
            pltpu.VMEM((2, 8, 128), F32),
            pltpu.VMEM((512, 128), BF16),
            pltpu.VMEM((128, 128), BF16),
            pltpu.VMEM((128, 128), BF16),
            pltpu.VMEM((128, 128), BF16),
            pltpu.VMEM((16, 128), BF16),
            pltpu.VMEM((8, 16, 128), BF16),
            dma((7,)),
            dma((12,)),
            dma((7,)),
            dma((7,)),
            dma((9,)),
            dma((9,)),
            dma((9,)),
            dma((9,)),
            dma((9,)),
            dma((8,)),
            dma((8,)),
        ],
        compiler_params=pltpu.CompilerParams(
            collective_id=0, has_side_effects=True, vmem_limit_bytes=24 << 20
        ),
    )(
        features.reshape(7, 256, 640),
        weight_x,
        weight_y,
        conv_weight,
        class_bias.reshape(1, 32),
    )
    return (
        outs[0].reshape(48, 32, 512),
        outs[1].reshape(24, 32, 128),
        outs[2].reshape(12, 32, 32),
        outs[3].reshape(6, 32, 64),
        outs[4].reshape(3, 32, 16),
    )


def solution(mesh):
    placed = (P("gx", None, "gy"), P("gx"), P("gy"), P(), P())
    return jax.shard_map(
        shards,
        mesh=mesh,
        in_specs=placed,
        out_specs=(
            P("gx", None, "gy"),
            P("gx", None, "gy"),
            P("gx", None, "gy"),
            P("gx", None, None),
            P("gx", None, None),
        ),
        check_vma=False,
    )
```

```python
import jax
import jax.numpy as jnp
from jax import lax
from jax.experimental import pallas as pl
from jax.experimental.pallas import tpu as pltpu
from jax.sharding import PartitionSpec as P

MESH = pl.DeviceIdType.MESH
F32 = jnp.float32
BF16 = jnp.bfloat16

CHUNKS = 6
ROWS = 256
PIECES = ((1, 0), (1, 1), (2, 0), (2, 1), (3, 0), (3, 1), (0, 0), (0, 1))
WAYS = (2, -2, 2, -2, -2, -2, 2, -2, 2)


def iota(shape, dim):
    return lax.broadcasted_iota(jnp.int32, shape, dim)


def one_hot(condition, value):
    return jnp.where(condition, value, 0.0).astype(BF16)


def dot(a, b):
    return jnp.dot(a, b, preferred_element_type=F32)


def device(x, y, z, core):
    return (z * 8 + (y // 4) * 4 + x, (y % 4) * 2 + core)


def kernel(
    features,
    weight_x_in,
    weight_y_in,
    conv_in,
    bias_in,
    out0,
    out1,
    level2,
    level3,
    level4,
    weight_x,
    weight_y,
    conv,
    bias,
    held,
    block,
    y_out,
    y_in,
    corner_out,
    corner_in,
    x_out,
    x_in,
    xw_out,
    xw_in,
    relay,
    relay_w,
    first_y,
    shares,
    pool1,
    pool2,
    pool3,
    pool4,
    own_third,
    all_third,
    load_sem,
    y_send,
    y_recv,
    x_send,
    x_recv,
    hop_send,
    hop_recv,
    on_send,
    third_send,
    third_recv,
):
    gx = lax.axis_index("gx")
    gy = lax.axis_index("gy")
    x, z, core = gx % 4, gx // 8, gy % 2
    y = (gx // 4) % 2 * 4 + gy // 2
    near = x < 3
    far = jnp.logical_and(x == 3, gx < 63)
    has_left = gx > 0
    has_up = gy > 0
    has_down = gy < 7

    def carries(way):
        source = (y - way + 8) % 8
        last = jnp.logical_and(z == 7, source >= 4)
        return jnp.logical_and(x == 0, jnp.logical_not(last))

    def carry_to(way):
        source = (y - way + 8) % 8
        return device(0, (source + 4) % 8, z + source // 4, core)

    far_in = jnp.logical_and(x == 0, has_left)

    loads = [
        pltpu.make_async_copy(features.at[i], held.at[i], load_sem.at[i])
        for i in range(7)
    ]
    loads.append(pltpu.make_async_copy(conv_in, conv, load_sem.at[7]))
    loads.append(pltpu.make_async_copy(bias_in, bias, load_sem.at[8]))
    loads.append(pltpu.make_async_copy(weight_x_in, weight_x, load_sem.at[9]))
    loads.append(pltpu.make_async_copy(weight_y_in, weight_y, load_sem.at[10]))
    for i in (7, 8, 9, 10, 6, 0, 1, 2, 3, 4, 5):
        loads[i].start()

    barrier = pltpu.get_barrier_semaphore()

    def greet(target):
        pl.semaphore_signal(barrier, inc=1, device_id=target, device_id_type=MESH)

    for way in (2, -2):

        @pl.when(carries(way))
        def _():
            greet(device(3, (y - way + 8) % 8, z, core))

        @pl.when(far_in)
        def _():
            before = z - jnp.where(y < 4, 1, 0)
            greet(device(0, (y + 4 + way) % 8, before, core))

    @pl.when(jnp.logical_and(has_left, x > 0))
    def _():
        greet((gx - 1, gy))

    for o in range(1, 8):
        greet((gx, (gy + o) % 8))

    for i in (7, 8, 9, 10):
        loads[i].wait()

    pick = (iota((ROWS, 32), 0) % 32) == iota((ROWS, 32), 1)
    spread = one_hot(pick, 1.0)
    dims = (((1,), (1,)), ((), ()))
    tall = lax.dot_general(spread, conv[...], dims, preferred_element_type=F32)
    wide = lax.dot_general(
        tall.astype(BF16), spread, dims, preferred_element_type=F32
    )
    same = iota((ROWS, ROWS), 0) // 32 == iota((ROWS, ROWS), 1) // 32
    block[...] = jnp.where(same, wide, 0.0).astype(BF16)
    bias_column = jnp.sum(jnp.where(pick, bias[...], 0.0), axis=1, keepdims=True)

    def logits(i):
        return (dot(block[...], held[i]) + bias_column).astype(BF16)

    lane_y = iota((8, 128), 1) // 16
    row = iota((8, 128), 0)
    wy_own = jnp.zeros((8, 128), F32)
    wy_last = jnp.zeros((8, 128), F32)
    wx_own = jnp.zeros((8, 128), F32)
    wx_last = jnp.zeros((8, 128), F32)
    for k in range(8):
        wy_own = jnp.where(lane_y == k, weight_y[k].astype(F32), wy_own)
        wy_last = jnp.where(lane_y == k, weight_y[32 + k].astype(F32), wy_last)
        wx_own = jnp.where(row == k, weight_x[k].astype(F32), wx_own)
        wx_last = jnp.where(row == k, weight_x[48 + k].astype(F32), wx_last)
    corner_out[ROWS:, :] = jnp.concatenate([wy_last, wy_last], axis=0).astype(BF16)
    xw_out[...] = jnp.concatenate([wx_last, wx_last], axis=0).astype(BF16)

    loads[6].wait()
    margin = logits(6)
    corner_out[:ROWS, :] = margin[:, 512:]
    for t in range(4):
        x_out[t] = margin[:, 128 * t : 128 * (t + 1)]

    peers = 7 + near.astype(jnp.int32) + 2 * far.astype(jnp.int32)
    for way in (2, -2):
        peers = peers + carries(way).astype(jnp.int32)
    pl.semaphore_wait(barrier, peers)

    def remote(src, dst, send, recv, target):
        return pltpu.make_async_remote_copy(
            src_ref=src,
            dst_ref=dst,
            send_sem=send,
            recv_sem=recv,
            device_id=target,
            device_id_type=MESH,
        )

    down = (gx, (gy + 1) % 8)
    corner_copy = remote(corner_out, corner_in, y_send.at[6], y_recv.at[6], down)
    y_copies = [
        remote(y_out.at[i], y_in.at[i], y_send.at[i], y_recv.at[i], down)
        for i in range(CHUNKS)
    ]

    def part(ref, h):
        t, half = PIECES[h]
        return ref.at[t, pl.ds(128 * half, 128)]

    def direct(h):
        target = ((gx + 1) % 64, gy)
        src, dst = (xw_out, xw_in) if h == 8 else (part(x_out, h), part(x_in, h))
        return remote(src, dst, x_send.at[h], x_recv.at[h], target)

    def hop(h):
        target = device(0, (y + WAYS[h] + 8) % 8, z, core)
        src, dst = (xw_out, relay_w) if h == 8 else (part(x_out, h), relay.at[h])
        return remote(src, dst, hop_send.at[h], hop_recv.at[h], target)

    def onward(h):
        target = carry_to(WAYS[h])
        src, dst = (relay_w, xw_in) if h == 8 else (relay.at[h], part(x_in, h))
        return remote(src, dst, on_send.at[h], x_recv.at[h], target)

    def send_x(pieces):
        @pl.when(near)
        def _():
            for h in pieces:
                direct(h).start()

        @pl.when(far)
        def _():
            for h in pieces:
                hop(h).start()

    @pl.when(has_down)
    def _():
        corner_copy.start()

    send_x((8, 0, 1, 2, 3, 4, 5))

    for i in range(CHUNKS):
        loads[i].wait()
        value = logits(i)
        y_out[i] = value[:, 512:]
        out0[i] = value[:, :512]

        @pl.when(has_down)
        def _():
            y_copies[i].start()

        if i == 3:
            @pl.when(has_up)
            def _():
                corner_copy.wait_recv()
                wy_up = corner_in[ROWS:, :].astype(F32)[:8]
                total = wy_own + wy_up
                own_share, up_share = wy_own / total, wy_up / total
                shares[0] = own_share
                shares[1] = up_share
                x_out[0] = (
                    x_out[0].astype(F32) * own_share[:1]
                    + corner_in[:ROWS, :].astype(F32) * up_share[:1]
                ).astype(BF16)

            send_x((6, 7))

    source, target = iota((512, 128), 0), iota((512, 128), 1)
    pool1[...] = one_hot(source // 32 * 8 + source % 16 // 2 == target, 0.125)
    source, target = iota((128, 128), 0), iota((128, 128), 1)
    pool2[...] = one_hot(source // 16 * 4 + source % 8 // 2 == target, 0.125)
    pool3[...] = one_hot(
        jnp.logical_and(
            source // 8 * 2 + source % 4 // 2 + gy * 8 == target, source < 32
        ),
        0.125,
    )
    pool4[...] = one_hot(jnp.logical_and(source // 4 == target, source < 64), 0.125)

    for h in (8, 0, 1, 2, 3, 4, 5, 6, 7):

        @pl.when(carries(WAYS[h]))
        def _():
            hop(h).wait_recv()
            onward(h).start()

    third = jnp.zeros((16, 128), F32)

    def mips(i, third):
        pooled = dot(out0[i], pool1[...]).reshape(4, 2, 32, 128)
        first = (pooled[:, 0] + pooled[:, 1]).astype(BF16).reshape(128, 128)
        out1[i] = first
        pooled = dot(first, pool2[...]).reshape(2, 2, 32, 128)
        second = (pooled[:, 0] + pooled[:, 1]).astype(BF16).reshape(64, 128)
        level2[pl.ds(64 * i, 64), :] = second[:, :32]
        pooled = dot(second, pool3[...])
        pooled = pooled[:32] + pooled[32:]
        third = third + pltpu.roll(pooled[:16], 8 * i, 1)
        return third + pltpu.roll(pooled[16:], 8 * (6 + i), 1)

    for i in range(1, CHUNKS):

        @pl.when(has_up)
        def _():
            y_copies[i].wait_recv()
            out0[i, :, :128] = (
                out0[i, :, :128].astype(F32) * shares[0, :1]
                + y_in[i].astype(F32) * shares[1, :1]
            ).astype(BF16)

        third = mips(i, third)

    first_y[...] = out0[0, :, :128].astype(F32)

    @pl.when(has_up)
    def _():
        y_copies[0].wait_recv()
        first_y[...] = first_y[...] * shares[0, :1] + y_in[0].astype(F32) * shares[1, :1]

    out0[0, :, :128] = first_y[...].astype(BF16)

    @pl.when(has_left)
    def _():
        for h in (8, 0, 1, 2, 3, 4, 5, 6, 7):
            direct(h).wait_recv()
        wx_left = xw_in[...].astype(F32)[:8]
        total = wx_own + wx_left
        own_share, left_share = wx_own / total, wx_left / total
        for a in range(8):
            rows = pl.ds(32 * a, 32)
            mine, theirs = own_share[a : a + 1], left_share[a : a + 1]
            for t in range(4):
                lanes = pl.ds(128 * t, 128)
                own = first_y[rows, :] if t == 0 else out0[0, rows, lanes].astype(F32)
                out0[0, rows, lanes] = (
                    own * mine + x_in[t, rows, :].astype(F32) * theirs
                ).astype(BF16)

    third = mips(0, third)

    own_third[...] = third.astype(BF16)
    third_copies = [
        remote(
            own_third,
            all_third.at[o],
            third_send.at[o],
            third_recv.at[o],
            (gx, (gy + o) % 8),
        )
        for o in range(1, 8)
    ]
    for copy in third_copies:
        copy.start()
    for copy in third_copies:
        copy.wait_recv()
    group = iota((16, 128), 1) // 8
    parts = [own_third[...].astype(F32)] + [
        all_third[o].astype(F32) for o in range(1, 8)
    ]
    rows = [None] * 12
    for q in range(12):
        owner = (group - q + 16) % 16
        value = jnp.zeros((16, 128), F32)
        for o in range(8):
            value = jnp.where(owner == (gy - o + 8) % 8, parts[o], value)
        half, i = q // 6, q % 6
        rows[2 * i + half] = pltpu.roll(value, (128 - 8 * q) % 128, 1)
    whole = jnp.concatenate(rows, axis=0).astype(BF16)
    level3[...] = whole[:, :64]
    pooled = dot(whole, pool4[...]).reshape(3, 2, 32, 128)
    fourth = pooled[:, 0] + pooled[:, 1]
    for t in range(3):
        level4[pl.ds(16 * t, 16), :] = fourth[t].T[:16].astype(BF16)

    for copy in third_copies:
        copy.wait_send()

    @pl.when(has_down)
    def _():
        corner_copy.wait_send()
        for i in range(CHUNKS):
            y_copies[i].wait_send()

    @pl.when(near)
    def _():
        for h in range(9):
            direct(h).wait_send()

    @pl.when(far)
    def _():
        for h in range(9):
            hop(h).wait_send()

    for h in range(9):

        @pl.when(carries(WAYS[h]))
        def _():
            onward(h).wait_send()


def store(*refs):
    sems = refs[10]
    copies = [pltpu.make_async_copy(refs[i], refs[5 + i], sems.at[i]) for i in range(5)]
    for copy in copies:
        copy.start()
    for copy in copies:
        copy.wait()


def shards(features, weight_x, weight_y, conv_weight, class_bias):
    vmem = pl.BlockSpec(memory_space=pltpu.VMEM)
    hbm = pl.BlockSpec(memory_space=pltpu.HBM)
    dma = pltpu.SemaphoreType.DMA
    shapes = (
        jax.ShapeDtypeStruct((6, 256, 512), BF16),
        jax.ShapeDtypeStruct((6, 128, 128), BF16),
        jax.ShapeDtypeStruct((384, 32), BF16),
        jax.ShapeDtypeStruct((192, 64), BF16),
        jax.ShapeDtypeStruct((48, 32), BF16),
    )
    outs = pl.pallas_call(
        kernel,
        name="blend",
        out_shape=shapes,
        in_specs=[hbm] * 5,
        out_specs=(vmem,) * 5,
        scratch_shapes=[
            pltpu.SMEM((56,), jnp.int32),
            pltpu.SMEM((40,), jnp.int32),
            pltpu.VMEM((32, 32), BF16),
            pltpu.VMEM((1, 32), F32),
            pltpu.VMEM((7, 256, 640), BF16),
            pltpu.VMEM((256, 256), BF16),
            pltpu.VMEM((6, 256, 128), BF16),
            pltpu.VMEM((6, 256, 128), BF16),
            pltpu.VMEM((272, 128), BF16),
            pltpu.VMEM((272, 128), BF16),
            pltpu.VMEM((4, 256, 128), BF16),
            pltpu.VMEM((4, 256, 128), BF16),
            pltpu.VMEM((16, 128), BF16),
            pltpu.VMEM((16, 128), BF16),
            pltpu.VMEM((8, 128, 128), BF16),
            pltpu.VMEM((16, 128), BF16),
            pltpu.VMEM((256, 128), F32),
            pltpu.VMEM((2, 8, 128), F32),
            pltpu.VMEM((512, 128), BF16),
            pltpu.VMEM((128, 128), BF16),
            pltpu.VMEM((128, 128), BF16),
            pltpu.VMEM((128, 128), BF16),
            pltpu.VMEM((16, 128), BF16),
            pltpu.VMEM((8, 16, 128), BF16),
            dma((11,)),
            dma((7,)),
            dma((7,)),
            dma((9,)),
            dma((9,)),
            dma((9,)),
            dma((9,)),
            dma((9,)),
            dma((8,)),
            dma((8,)),
        ],
        compiler_params=pltpu.CompilerParams(
            collective_id=0, has_side_effects=True, vmem_limit_bytes=24 << 20
        ),
    )(
        *(
            pltpu.with_memory_space_constraint(value, pltpu.HBM)
            for value in (
                features.reshape(7, 256, 640),
                weight_x,
                weight_y,
                conv_weight,
                class_bias.reshape(1, 32),
            )
        )
    )
    outs = pl.pallas_call(
        store,
        name="store",
        out_shape=shapes,
        in_specs=[pl.BlockSpec(memory_space=pl.ANY)] * 5,
        out_specs=(hbm,) * 5,
        scratch_shapes=[dma((5,))],
        compiler_params=pltpu.CompilerParams(vmem_limit_bytes=1 << 20),
    )(*outs)
    return (
        outs[0].reshape(48, 32, 512),
        outs[1].reshape(24, 32, 128),
        outs[2].reshape(12, 32, 32),
        outs[3].reshape(6, 32, 64),
        outs[4].reshape(3, 16, 32).transpose(0, 2, 1),
    )


def solution(mesh):
    placed = (P("gx", None, "gy"), P("gx"), P("gy"), P(), P())
    return jax.shard_map(
        shards,
        mesh=mesh,
        in_specs=placed,
        out_specs=(
            P("gx", None, "gy"),
            P("gx", None, "gy"),
            P("gx", None, "gy"),
            P("gx", None, None),
            P("gx", None, None),
        ),
        check_vma=False,
    )
```

```python
import jax
import jax.numpy as jnp
from jax import lax
from jax.experimental import pallas as pl
from jax.experimental.pallas import tpu as pltpu
from jax.sharding import PartitionSpec as P

MESH = pl.DeviceIdType.MESH
F32 = jnp.float32
BF16 = jnp.bfloat16

CHUNKS = 6
ROWS = 256
PIECES = ((1, 0), (1, 1), (2, 0), (2, 1), (3, 0), (3, 1), (0, 0), (0, 1))
POOLED = 8
VIA = (0, 0, 0, 1, 1, None, None, None, None)


def iota(shape, dim):
    return lax.broadcasted_iota(jnp.int32, shape, dim)


def one_hot(condition, value):
    return jnp.where(condition, value, 0.0).astype(BF16)


def dot(a, b):
    return jnp.dot(a, b, preferred_element_type=F32)


def device(x, y, z, core):
    return (z * 8 + (y // 4) * 4 + x, (y % 4) * 2 + core)


def kernel(
    features,
    weight_x_in,
    weight_y_in,
    conv_in,
    bias_in,
    out0,
    out1,
    level2,
    level3,
    level4,
    weight_x,
    weight_y,
    conv,
    bias,
    held,
    block,
    y_out,
    y_in,
    corner_out,
    corner_in,
    x_out,
    x_in,
    pooled_out,
    pooled_in,
    relay,
    first_y,
    shares,
    pool1,
    pool2,
    pool3,
    pool4,
    pool_row,
    own_third,
    all_third,
    load_sem,
    y_send,
    y_recv,
    x_send,
    x_recv,
    hop_send,
    hop_recv,
    on_send,
    third_send,
    third_recv,
):
    gx = lax.axis_index("gx")
    gy = lax.axis_index("gy")
    x, z, core = gx % 4, gx // 8, gy % 2
    y = (gx // 4) % 2 * 4 + gy // 2
    near = x < 3
    far = jnp.logical_and(x == 3, gx < 63)
    has_left = gx > 0
    has_up = gy > 0
    has_down = gy < 7
    far_in = jnp.logical_and(x == 0, has_left)
    passing = jnp.logical_not(jnp.logical_and(z == 7, y >= 4))

    def carries(via):
        return jnp.logical_and(x == via, passing)

    names = (
        (conv_in, conv),
        (bias_in, bias),
        (weight_x_in, weight_x),
        (weight_y_in, weight_y),
    )
    loads = [
        pltpu.make_async_copy(features.at[i], held.at[i], load_sem.at[i])
        for i in range(7)
    ]
    small = [
        pltpu.make_async_copy(src, dst, load_sem.at[7 + i])
        for i, (src, dst) in enumerate(names)
    ]
    for copy in small:
        copy.start()
    for i in (6, 0, 1, 2, 3, 4, 5):
        loads[i].start()

    barrier = pltpu.get_barrier_semaphore()

    def greet(target):
        pl.semaphore_signal(barrier, inc=1, device_id=target, device_id_type=MESH)

    @pl.when(far_in)
    def _():
        before = z - jnp.where(y < 4, 1, 0)
        for via in (0, 1):
            greet(device(via, (y + 4) % 8, before, core))

    @pl.when(has_left)
    def _():
        greet((gx - 1, gy))

    for via in (0, 1):

        @pl.when(carries(via))
        def _():
            greet(device(3, y, z, core))

    for o in range(1, 8):
        greet((gx, (gy + o) % 8))

    for copy in small:
        copy.wait()

    pick = (iota((ROWS, 32), 0) % 32) == iota((ROWS, 32), 1)
    spread = one_hot(pick, 1.0)
    dims = (((1,), (1,)), ((), ()))
    tall = lax.dot_general(spread, conv[...], dims, preferred_element_type=F32)
    wide = lax.dot_general(
        tall.astype(BF16), spread, dims, preferred_element_type=F32
    )
    same = iota((ROWS, ROWS), 0) // 32 == iota((ROWS, ROWS), 1) // 32
    block[...] = jnp.where(same, wide, 0.0).astype(BF16)
    bias_column = jnp.sum(jnp.where(pick, bias[...], 0.0), axis=1, keepdims=True)

    def logits(i):
        return (dot(block[...], held[i]) + bias_column).astype(BF16)

    lane_y = iota((8, 128), 1) // 16
    row = iota((8, 128), 0)
    nothing = jnp.zeros((8, 128), F32)
    wy_own, wy_last, wx_own, wx_last, wx_own_lane, wx_last_lane = (nothing,) * 6
    for k in range(8):
        own, last = weight_y[k].astype(F32), weight_y[32 + k].astype(F32)
        wy_own = jnp.where(lane_y == k, own, wy_own)
        wy_last = jnp.where(lane_y == k, last, wy_last)
        own, last = weight_x[k].astype(F32), weight_x[48 + k].astype(F32)
        wx_own = jnp.where(row == k, own, wx_own)
        wx_last = jnp.where(row == k, last, wx_last)
        wx_own_lane = jnp.where(lane_y == k, own, wx_own_lane)
        wx_last_lane = jnp.where(lane_y == k, last, wx_last_lane)
    corner_out[ROWS:, :] = jnp.concatenate([wy_last, wy_last], axis=0).astype(BF16)
    pooled_out[16:, :] = jnp.concatenate([wx_last, wx_last_lane], axis=0).astype(BF16)

    loads[6].wait()
    margin = logits(6)
    corner_out[:ROWS, :] = margin[:, 512:]
    for t in range(4):
        x_out[t] = margin[:, 128 * t : 128 * (t + 1)]

    for i in range(CHUNKS):
        loads[i].wait()
        value = logits(i)
        y_out[i] = value[:, 512:]
        out0[i] = value[:, :512]

    peers = 7 + near.astype(jnp.int32) + 3 * far.astype(jnp.int32)
    for via in (0, 1):
        peers = peers + carries(via).astype(jnp.int32)
    pl.semaphore_wait(barrier, peers)

    def remote(src, dst, send, recv, target):
        return pltpu.make_async_remote_copy(
            src_ref=src,
            dst_ref=dst,
            send_sem=send,
            recv_sem=recv,
            device_id=target,
            device_id_type=MESH,
        )

    down = (gx, (gy + 1) % 8)
    corner_copy = remote(corner_out, corner_in, y_send.at[6], y_recv.at[6], down)
    y_copies = [
        remote(y_out.at[i], y_in.at[i], y_send.at[i], y_recv.at[i], down)
        for i in range(CHUNKS)
    ]

    def part(ref, h):
        t, half = PIECES[h]
        return ref.at[t, pl.ds(128 * half, 128)]

    def direct(h):
        target = ((gx + 1) % 64, gy)
        if h == POOLED:
            src, dst = pooled_out, pooled_in
        else:
            src, dst = part(x_out, h), part(x_in, h)
        return remote(src, dst, x_send.at[h], x_recv.at[h], target)

    def hop(h):
        target = device(VIA[h], y, z, core)
        return remote(
            part(x_out, h), relay.at[h], hop_send.at[h], hop_recv.at[h], target
        )

    def onward(h):
        target = device(0, (y + 4) % 8, z + y // 4, core)
        return remote(
            relay.at[h], part(x_in, h), on_send.at[h], x_recv.at[h], target
        )

    def send_x(pieces):
        @pl.when(near)
        def _():
            for h in pieces:
                direct(h).start()

        @pl.when(far)
        def _():
            for h in pieces:
                (direct if VIA[h] is None else hop)(h).start()

    @pl.when(has_down)
    def _():
        corner_copy.start()

    send_x((0, 1, 2, 3, 4, 5))

    @pl.when(has_down)
    def _():
        for i in (1, 2, 3, 4, 5, 0):
            y_copies[i].start()

    source, target = iota((512, 128), 0), iota((512, 128), 1)
    pool1[...] = one_hot(source // 32 * 8 + source % 16 // 2 == target, 0.125)
    pool_row[...] = one_hot(
        source // 128 * 2 + source % 16 // 8 == target % 8, 1.0 / 512
    )
    source, target = iota((128, 128), 0), iota((128, 128), 1)
    pool2[...] = one_hot(source // 16 * 4 + source % 8 // 2 == target, 0.125)
    pool4[...] = one_hot(jnp.logical_and(source // 4 == target, source < 64), 0.125)
    pool3[...] = one_hot(
        jnp.logical_and(source // 8 * 2 + source % 4 // 2 == target % 8, source < 32),
        0.125,
    )

    for via in (0, 1):

        @pl.when(carries(via))
        def _():
            for h in range(9):
                if VIA[h] == via:
                    hop(h).wait_recv()
                    onward(h).start()

    @pl.when(has_up)
    def _():
        corner_copy.wait_recv()
        wy_up = corner_in[ROWS:, :].astype(F32)[:8]
        total = wy_own + wy_up
        own_share, up_share = wy_own / total, wy_up / total
        shares[0] = own_share
        shares[1] = up_share
        x_out[0] = (
            x_out[0].astype(F32) * own_share[:1]
            + corner_in[:ROWS, :].astype(F32) * up_share[:1]
        ).astype(BF16)

    group = iota((16, 128), 1) // 8

    def pool_rows(tiles):
        total = dot(tiles[0], pool_row[:128])
        for t in range(1, 4):
            total = total + dot(tiles[t], pool_row[128 * t : 128 * (t + 1)])
        return total

    send_x((6, 7))
    rows = pool_rows([x_out[t] for t in range(4)])
    value = jnp.zeros((16, 128), F32)
    for g in range(16):
        value = jnp.where(group == g, rows[16 * g : 16 * (g + 1)], value)
    pooled_out[:16, :] = value.astype(BF16)
    send_x((POOLED,))

    third = jnp.zeros((16, 128), F32)

    def place(third, i, value):
        third = jnp.where(group == (gy + i) % 16, value[:16], third)
        return jnp.where(group == (gy + 6 + i) % 16, value[16:], third)

    def mips(i):
        pooled = dot(out0[i], pool1[...]).reshape(4, 2, 32, 128)
        first = (pooled[:, 0] + pooled[:, 1]).astype(BF16).reshape(128, 128)
        out1[i] = first
        pooled = dot(first, pool2[...]).reshape(2, 2, 32, 128)
        second = (pooled[:, 0] + pooled[:, 1]).astype(BF16).reshape(64, 128)
        level2[pl.ds(64 * i, 64), :] = second[:, :32]
        return second

    for i in range(1, CHUNKS):

        @pl.when(has_up)
        def _():
            y_copies[i].wait_recv()
            out0[i, :, :128] = (
                out0[i, :, :128].astype(F32) * shares[0, :1]
                + y_in[i].astype(F32) * shares[1, :1]
            ).astype(BF16)

        pooled = dot(mips(i), pool3[...])
        third = place(third, i, pooled[:32] + pooled[32:])

    first_y[...] = out0[0, :, :128].astype(F32)

    @pl.when(has_up)
    def _():
        y_copies[0].wait_recv()
        first_y[...] = first_y[...] * shares[0, :1] + y_in[0].astype(F32) * shares[1, :1]

    @pl.when(has_left)
    def _():
        direct(POOLED).wait_recv()

    @pl.when(jnp.logical_not(has_left))
    def _():
        pooled_in[...] = jnp.zeros((32, 128), BF16)

    left = pooled_in[...].astype(F32)
    wx_left, wx_left_lane = left[16:24], left[24:]
    own_share = wx_own / (wx_own + wx_left)
    left_share = wx_left / (wx_own + wx_left)
    rows = pool_rows(
        [first_y[...].astype(BF16)]
        + [out0[0, :, 128 * t : 128 * (t + 1)] for t in range(1, 4)]
    )
    value = jnp.zeros((32, 128), F32)
    for a in range(8):
        value = value + rows[32 * a : 32 * (a + 1)] * own_share[a : a + 1]
    other = left[:16] * (wx_left_lane / (wx_own_lane + wx_left_lane))[:1]
    for shift in (64, 32, 16):
        other = other + pltpu.roll(other, shift, 1)
    turned = pltpu.roll(other, 8, 1)
    even = group % 2 == 0
    other = jnp.concatenate(
        [jnp.where(even, other, turned), jnp.where(even, turned, other)], axis=0
    )
    third = place(third, 0, value + other)

    own_third[...] = third.astype(BF16)
    third_copies = [
        remote(
            own_third,
            all_third.at[o],
            third_send.at[o],
            third_recv.at[o],
            (gx, (gy + o) % 8),
        )
        for o in range(1, 8)
    ]
    for copy in third_copies:
        copy.start()

    @pl.when(jnp.logical_not(has_left))
    def _():
        out0[0, :, :128] = first_y[...].astype(BF16)

    @pl.when(has_left)
    def _():
        for h in range(8):
            direct(h).wait_recv()
        for a in range(8):
            rows = pl.ds(32 * a, 32)
            mine, theirs = own_share[a : a + 1], left_share[a : a + 1]
            for t in range(4):
                lanes = pl.ds(128 * t, 128)
                own = first_y[rows, :] if t == 0 else out0[0, rows, lanes].astype(F32)
                out0[0, rows, lanes] = (
                    own * mine + x_in[t, rows, :].astype(F32) * theirs
                ).astype(BF16)

    mips(0)

    for copy in third_copies:
        copy.wait_recv()
    parts = [own_third[...].astype(F32)] + [
        all_third[o].astype(F32) for o in range(1, 8)
    ]
    rows = [None] * 12
    for q in range(12):
        owner = (group - q + 16) % 16
        value = jnp.zeros((16, 128), F32)
        for o in range(8):
            value = jnp.where(owner == (gy - o + 8) % 8, parts[o], value)
        half, i = q // 6, q % 6
        rows[2 * i + half] = pltpu.roll(value, (128 - 8 * q) % 128, 1)
    whole = jnp.concatenate(rows, axis=0).astype(BF16)
    level3[...] = whole[:, :64]
    pooled = dot(whole, pool4[...]).reshape(3, 2, 32, 128)
    fourth = pooled[:, 0] + pooled[:, 1]
    for t in range(3):
        level4[pl.ds(16 * t, 16), :] = fourth[t].T[:16].astype(BF16)

    for copy in third_copies:
        copy.wait_send()

    @pl.when(has_down)
    def _():
        corner_copy.wait_send()
        for i in range(CHUNKS):
            y_copies[i].wait_send()

    @pl.when(near)
    def _():
        for h in range(9):
            direct(h).wait_send()

    @pl.when(far)
    def _():
        for h in range(9):
            (direct if VIA[h] is None else hop)(h).wait_send()

    for via in (0, 1):

        @pl.when(carries(via))
        def _():
            for h in range(9):
                if VIA[h] == via:
                    onward(h).wait_send()


def store(*refs):
    sems = refs[10]
    copies = [pltpu.make_async_copy(refs[i], refs[5 + i], sems.at[i]) for i in range(5)]
    for copy in copies:
        copy.start()
    for copy in copies:
        copy.wait()


def shards(features, weight_x, weight_y, conv_weight, class_bias):
    vmem = pl.BlockSpec(memory_space=pltpu.VMEM)
    hbm = pl.BlockSpec(memory_space=pltpu.HBM)
    dma = pltpu.SemaphoreType.DMA
    shapes = (
        jax.ShapeDtypeStruct((6, 256, 512), BF16),
        jax.ShapeDtypeStruct((6, 128, 128), BF16),
        jax.ShapeDtypeStruct((384, 32), BF16),
        jax.ShapeDtypeStruct((192, 64), BF16),
        jax.ShapeDtypeStruct((48, 32), BF16),
    )
    outs = pl.pallas_call(
        kernel,
        name="blend",
        out_shape=shapes,
        in_specs=[hbm] * 5,
        out_specs=(vmem,) * 5,
        scratch_shapes=[
            pltpu.SMEM((56,), jnp.int32),
            pltpu.SMEM((40,), jnp.int32),
            pltpu.VMEM((32, 32), BF16),
            pltpu.VMEM((1, 32), F32),
            pltpu.VMEM((7, 256, 640), BF16),
            pltpu.VMEM((256, 256), BF16),
            pltpu.VMEM((6, 256, 128), BF16),
            pltpu.VMEM((6, 256, 128), BF16),
            pltpu.VMEM((272, 128), BF16),
            pltpu.VMEM((272, 128), BF16),
            pltpu.VMEM((4, 256, 128), BF16),
            pltpu.VMEM((4, 256, 128), BF16),
            pltpu.VMEM((32, 128), BF16),
            pltpu.VMEM((32, 128), BF16),
            pltpu.VMEM((5, 128, 128), BF16),
            pltpu.VMEM((256, 128), F32),
            pltpu.VMEM((2, 8, 128), F32),
            pltpu.VMEM((512, 128), BF16),
            pltpu.VMEM((128, 128), BF16),
            pltpu.VMEM((128, 128), BF16),
            pltpu.VMEM((128, 128), BF16),
            pltpu.VMEM((512, 128), BF16),
            pltpu.VMEM((16, 128), BF16),
            pltpu.VMEM((8, 16, 128), BF16),
            dma((11,)),
            dma((7,)),
            dma((7,)),
            dma((9,)),
            dma((9,)),
            dma((5,)),
            dma((5,)),
            dma((5,)),
            dma((8,)),
            dma((8,)),
        ],
        compiler_params=pltpu.CompilerParams(
            collective_id=0, has_side_effects=True, vmem_limit_bytes=24 << 20
        ),
    )(
        *(
            pltpu.with_memory_space_constraint(value, pltpu.HBM)
            for value in (
                features.reshape(7, 256, 640),
                weight_x,
                weight_y,
                conv_weight,
                class_bias.reshape(1, 32),
            )
        )
    )
    outs = pl.pallas_call(
        store,
        name="store",
        out_shape=shapes,
        in_specs=[pl.BlockSpec(memory_space=pl.ANY)] * 5,
        out_specs=(hbm,) * 5,
        scratch_shapes=[dma((5,))],
        compiler_params=pltpu.CompilerParams(vmem_limit_bytes=1 << 20),
    )(*outs)
    return (
        outs[0].reshape(48, 32, 512),
        outs[1].reshape(24, 32, 128),
        outs[2].reshape(12, 32, 32),
        outs[3].reshape(6, 32, 64),
        outs[4].reshape(3, 16, 32).transpose(0, 2, 1),
    )


def solution(mesh):
    placed = (P("gx", None, "gy"), P("gx"), P("gy"), P(), P())
    return jax.shard_map(
        shards,
        mesh=mesh,
        in_specs=placed,
        out_specs=(
            P("gx", None, "gy"),
            P("gx", None, "gy"),
            P("gx", None, "gy"),
            P("gx", None, None),
            P("gx", None, None),
        ),
        check_vma=False,
    )
```

```python
import jax
import jax.numpy as jnp
from jax import lax
from jax.experimental import pallas as pl
from jax.experimental.pallas import tpu as pltpu
from jax.sharding import PartitionSpec as P

MESH = pl.DeviceIdType.MESH
F32 = jnp.float32
BF16 = jnp.bfloat16

CHUNKS = 6
ROWS = 256
PIECES = ((1, 0), (1, 1), (2, 0), (2, 1), (3, 0), (3, 1), (0, 0), (0, 1))
POOLED = 8
VIA = (0, 0, 0, 1, 1, None, None, None, None)


def iota(shape, dim):
    return lax.broadcasted_iota(jnp.int32, shape, dim)


def one_hot(condition, value):
    return jnp.where(condition, value, 0.0).astype(BF16)


def dot(a, b):
    return jnp.dot(a, b, preferred_element_type=F32)


def device(x, y, z, core):
    return (z * 8 + (y // 4) * 4 + x, (y % 4) * 2 + core)


def kernel(
    features,
    weight_x_in,
    weight_y_in,
    conv_in,
    bias_in,
    out0,
    out1,
    level2,
    level3,
    level4,
    weight_x,
    weight_y,
    conv,
    bias,
    held,
    block,
    y_out,
    y_in,
    corner_out,
    corner_in,
    x_out,
    x_in,
    pooled_out,
    pooled_in,
    relay,
    first_y,
    shares,
    pool1,
    pool2,
    pool3,
    pool4,
    pool_row,
    own_third,
    all_third,
    load_sem,
    y_send,
    y_recv,
    x_send,
    x_recv,
    hop_send,
    hop_recv,
    on_send,
    third_send,
    third_recv,
    told,
):
    gx = lax.axis_index("gx")
    gy = lax.axis_index("gy")
    x, z, core = gx % 4, gx // 8, gy % 2
    y = (gx // 4) % 2 * 4 + gy // 2
    near = x < 3
    far = jnp.logical_and(x == 3, gx < 63)
    has_left = gx > 0
    has_up = gy > 0
    has_down = gy < 7
    far_in = jnp.logical_and(x == 0, has_left)
    passing = jnp.logical_not(jnp.logical_and(z == 7, y >= 4))

    def carries(via):
        return jnp.logical_and(x == via, passing)

    names = (
        (conv_in, conv),
        (bias_in, bias),
        (weight_x_in, weight_x),
        (weight_y_in, weight_y),
    )
    loads = [
        pltpu.make_async_copy(features.at[i], held.at[i], load_sem.at[i])
        for i in range(7)
    ]
    small = [
        pltpu.make_async_copy(src, dst, load_sem.at[7 + i])
        for i, (src, dst) in enumerate(names)
    ]
    for copy in small:
        copy.start()
    for i in (6, 0, 1, 2, 3, 4, 5):
        loads[i].start()

    barrier = pltpu.get_barrier_semaphore()

    def tell(semaphore, target):
        pl.semaphore_signal(semaphore, inc=1, device_id=target, device_id_type=MESH)

    middle_y = (y + 6) % 8
    middle = jnp.logical_and(
        x == 0, jnp.logical_not(jnp.logical_and(z == 7, middle_y >= 4))
    )

    for via in (0, 1):

        @pl.when(carries(via))
        def _():
            tell(barrier, device(3, y, z, core))
            tell(barrier, device(0, (y + 2) % 8, z, core))

    @pl.when(far)
    def _():
        tell(barrier, device(0, (y + 2) % 8, z, core))

    @pl.when(far_in)
    def _():
        tell(barrier, device(0, middle_y, z - jnp.where(y < 4, 1, 0), core))

    @pl.when(x > 0)
    def _():
        tell(barrier, (gx - 1, gy))

    def tell_group(semaphore, steps):
        @pl.when(gy >= steps)
        def _():
            tell(semaphore, (gx, gy - steps))

        @pl.when(gy + steps < 8)
        def _():
            tell(semaphore, (gx, gy + steps))

    def in_group(steps):
        return (gy >= steps).astype(jnp.int32) + (gy + steps < 8).astype(jnp.int32)

    tell_group(barrier, 1)

    for copy in small:
        copy.wait()

    pick = (iota((ROWS, 32), 0) % 32) == iota((ROWS, 32), 1)
    spread = one_hot(pick, 1.0)
    dims = (((1,), (1,)), ((), ()))
    tall = lax.dot_general(spread, conv[...], dims, preferred_element_type=F32)
    wide = lax.dot_general(
        tall.astype(BF16), spread, dims, preferred_element_type=F32
    )
    same = iota((ROWS, ROWS), 0) // 32 == iota((ROWS, ROWS), 1) // 32
    block[...] = jnp.where(same, wide, 0.0).astype(BF16)
    bias_column = jnp.sum(jnp.where(pick, bias[...], 0.0), axis=1, keepdims=True)

    def logits(i, lanes):
        return (dot(block[...], held[i, :, lanes]) + bias_column).astype(BF16)

    lane_y = iota((8, 128), 1) // 16
    row = iota((8, 128), 0)
    nothing = jnp.zeros((8, 128), F32)
    wy_own, wy_last, wx_own, wx_last, wx_own_lane, wx_last_lane = (nothing,) * 6
    for k in range(8):
        own, last = weight_y[k].astype(F32), weight_y[32 + k].astype(F32)
        wy_own = jnp.where(lane_y == k, own, wy_own)
        wy_last = jnp.where(lane_y == k, last, wy_last)
        own, last = weight_x[k].astype(F32), weight_x[48 + k].astype(F32)
        wx_own = jnp.where(row == k, own, wx_own)
        wx_last = jnp.where(row == k, last, wx_last)
        wx_own_lane = jnp.where(lane_y == k, own, wx_own_lane)
        wx_last_lane = jnp.where(lane_y == k, last, wx_last_lane)
    corner_out[ROWS:, :] = jnp.concatenate([wy_last, wy_last], axis=0).astype(BF16)
    pooled_out[16:, :] = jnp.concatenate([wx_last, wx_last_lane], axis=0).astype(BF16)

    loads[6].wait()
    margin = logits(6, slice(0, 640))
    corner_out[:ROWS, :] = margin[:, 512:]
    for t in range(4):
        x_out[t] = margin[:, 128 * t : 128 * (t + 1)]

    for i in range(CHUNKS):
        loads[i].wait()
        y_out[i] = logits(i, slice(512, 640))

    peers = in_group(1) + near.astype(jnp.int32)
    peers = peers + 2 * far.astype(jnp.int32) + 4 * middle.astype(jnp.int32)
    pl.semaphore_wait(barrier, peers)

    @pl.when(middle)
    def _():
        for source_x in (0, 1, 3):
            tell(told.at[0], device(source_x, middle_y, z, core))

    tell_group(told.at[1], 1)

    def remote(src, dst, send, recv, target):
        return pltpu.make_async_remote_copy(
            src_ref=src,
            dst_ref=dst,
            send_sem=send,
            recv_sem=recv,
            device_id=target,
            device_id_type=MESH,
        )

    down = (gx, (gy + 1) % 8)
    corner_copy = remote(corner_out, corner_in, y_send.at[6], y_recv.at[6], down)
    y_copies = [
        remote(y_out.at[i], y_in.at[i], y_send.at[i], y_recv.at[i], down)
        for i in range(CHUNKS)
    ]

    def part(ref, h):
        t, half = PIECES[h]
        return ref.at[t, pl.ds(128 * half, 128)]

    def direct(h):
        target = ((gx + 1) % 64, gy)
        if h == POOLED:
            src, dst = pooled_out, pooled_in
        else:
            src, dst = part(x_out, h), part(x_in, h)
        return remote(src, dst, x_send.at[h], x_recv.at[h], target)

    def hop(h):
        target = device(VIA[h], y, z, core)
        return remote(
            part(x_out, h), relay.at[h], hop_send.at[h], hop_recv.at[h], target
        )

    def onward(h):
        target = device(0, (y + 4) % 8, z + y // 4, core)
        return remote(
            relay.at[h], part(x_in, h), on_send.at[h], x_recv.at[h], target
        )

    def send_x(pieces):
        @pl.when(near)
        def _():
            for h in pieces:
                direct(h).start()

        @pl.when(far)
        def _():
            for h in pieces:
                (direct if VIA[h] is None else hop)(h).start()

    @pl.when(has_down)
    def _():
        corner_copy.start()

    send_x((0, 1, 2, 3, 4))

    @pl.when(has_down)
    def _():
        for i in (1, 2, 3, 4, 5, 0):
            y_copies[i].start()

    for i in range(CHUNKS):
        out0[i] = logits(i, slice(0, 512))

    pl.semaphore_wait(told.at[1], in_group(1))
    tell_group(told.at[2], 2)

    source, target = iota((512, 128), 0), iota((512, 128), 1)
    pool1[...] = one_hot(source // 32 * 8 + source % 16 // 2 == target, 0.125)
    pool_row[...] = one_hot(
        source // 128 * 2 + source % 16 // 8 == target % 8, 1.0 / 512
    )
    source, target = iota((128, 128), 0), iota((128, 128), 1)
    pool2[...] = one_hot(source // 16 * 4 + source % 8 // 2 == target, 0.125)
    pool4[...] = one_hot(jnp.logical_and(source // 4 == target, source < 64), 0.125)
    pool3[...] = one_hot(
        jnp.logical_and(source // 8 * 2 + source % 4 // 2 == target % 8, source < 32),
        0.125,
    )

    @pl.when(far)
    def _():
        pl.semaphore_wait(told.at[0], 1)

    send_x((5,))

    for via in (0, 1):

        @pl.when(carries(via))
        def _():
            pl.semaphore_wait(told.at[0], 1)
            for h in range(9):
                if VIA[h] == via:
                    hop(h).wait_recv()
                    onward(h).start()

    def pool_rows(tiles):
        return sum(dot(v, pool_row[128 * t : 128 * (t + 1)]) for t, v in tiles)

    group = iota((16, 128), 1) // 8
    rows = pool_rows([(t, x_out[t]) for t in range(1, 4)])

    @pl.when(has_up)
    def _():
        corner_copy.wait_recv()
        wy_up = corner_in[ROWS:, :].astype(F32)[:8]
        total = wy_own + wy_up
        own_share, up_share = wy_own / total, wy_up / total
        shares[0] = own_share
        shares[1] = up_share
        x_out[0] = (
            x_out[0].astype(F32) * own_share[:1]
            + corner_in[:ROWS, :].astype(F32) * up_share[:1]
        ).astype(BF16)

    rows = rows + pool_rows([(0, x_out[0])])
    value = jnp.zeros((16, 128), F32)
    for g in range(16):
        value = jnp.where(group == g, rows[16 * g : 16 * (g + 1)], value)
    pooled_out[:16, :] = value.astype(BF16)
    send_x((POOLED, 6, 7))

    pl.semaphore_wait(told.at[2], in_group(2))
    tell_group(told.at[3], 4)

    third = jnp.zeros((16, 128), F32)

    def place(third, i, value):
        third = jnp.where(group == (gy + i) % 16, value[:16], third)
        return jnp.where(group == (gy + 6 + i) % 16, value[16:], third)

    def mips(i):
        pooled = dot(out0[i], pool1[...]).reshape(4, 2, 32, 128)
        first = (pooled[:, 0] + pooled[:, 1]).astype(BF16).reshape(128, 128)
        out1[i] = first
        pooled = dot(first, pool2[...]).reshape(2, 2, 32, 128)
        second = (pooled[:, 0] + pooled[:, 1]).astype(BF16).reshape(64, 128)
        level2[pl.ds(64 * i, 64), :] = second[:, :32]
        return second

    for i in range(1, CHUNKS):

        @pl.when(has_up)
        def _():
            y_copies[i].wait_recv()
            out0[i, :, :128] = (
                out0[i, :, :128].astype(F32) * shares[0, :1]
                + y_in[i].astype(F32) * shares[1, :1]
            ).astype(BF16)

        pooled = dot(mips(i), pool3[...])
        third = place(third, i, pooled[:32] + pooled[32:])

    first_y[...] = out0[0, :, :128].astype(F32)

    @pl.when(has_up)
    def _():
        y_copies[0].wait_recv()
        first_y[...] = first_y[...] * shares[0, :1] + y_in[0].astype(F32) * shares[1, :1]

    @pl.when(has_left)
    def _():
        direct(POOLED).wait_recv()

    @pl.when(jnp.logical_not(has_left))
    def _():
        pooled_in[...] = jnp.zeros((32, 128), BF16)

    left = pooled_in[...].astype(F32)
    wx_left, wx_left_lane = left[16:24], left[24:]
    own_share = wx_own / (wx_own + wx_left)
    left_share = wx_left / (wx_own + wx_left)
    rows = pool_rows(
        [(0, first_y[...].astype(BF16))]
        + [(t, out0[0, :, 128 * t : 128 * (t + 1)]) for t in range(1, 4)]
    )
    value = jnp.zeros((32, 128), F32)
    for a in range(8):
        value = value + rows[32 * a : 32 * (a + 1)] * own_share[a : a + 1]
    other = left[:16] * (wx_left_lane / (wx_own_lane + wx_left_lane))[:1]
    for shift in (64, 32, 16):
        other = other + pltpu.roll(other, shift, 1)
    turned = pltpu.roll(other, 8, 1)
    even = group % 2 == 0
    other = jnp.concatenate(
        [jnp.where(even, other, turned), jnp.where(even, turned, other)], axis=0
    )
    third = place(third, 0, value + other)

    pl.semaphore_wait(told.at[3], 1)
    own_third[...] = third.astype(BF16)
    third_copies = [
        remote(
            own_third,
            all_third.at[o],
            third_send.at[o],
            third_recv.at[o],
            (gx, (gy + o) % 8),
        )
        for o in range(1, 8)
    ]
    for copy in third_copies:
        copy.start()

    @pl.when(jnp.logical_not(has_left))
    def _():
        out0[0, :, :128] = first_y[...].astype(BF16)

    @pl.when(has_left)
    def _():
        for h in range(8):
            direct(h).wait_recv()
        for a in range(8):
            rows = pl.ds(32 * a, 32)
            mine, theirs = own_share[a : a + 1], left_share[a : a + 1]
            for t in range(4):
                lanes = pl.ds(128 * t, 128)
                own = first_y[rows, :] if t == 0 else out0[0, rows, lanes].astype(F32)
                out0[0, rows, lanes] = (
                    own * mine + x_in[t, rows, :].astype(F32) * theirs
                ).astype(BF16)

    mips(0)

    for copy in third_copies:
        copy.wait_recv()
    parts = [own_third[...].astype(F32)] + [
        all_third[o].astype(F32) for o in range(1, 8)
    ]
    rows = [None] * 12
    for q in range(12):
        owner = (group - q + 16) % 16
        value = jnp.zeros((16, 128), F32)
        for o in range(8):
            value = jnp.where(owner == (gy - o + 8) % 8, parts[o], value)
        half, i = q // 6, q % 6
        rows[2 * i + half] = pltpu.roll(value, (128 - 8 * q) % 128, 1)
    whole = jnp.concatenate(rows, axis=0).astype(BF16)
    level3[...] = whole[:, :64]
    pooled = dot(whole, pool4[...]).reshape(3, 2, 32, 128)
    fourth = pooled[:, 0] + pooled[:, 1]
    for t in range(3):
        level4[pl.ds(16 * t, 16), :] = fourth[t].T[:16].astype(BF16)

    for copy in third_copies:
        copy.wait_send()

    @pl.when(has_down)
    def _():
        corner_copy.wait_send()
        for i in range(CHUNKS):
            y_copies[i].wait_send()

    @pl.when(near)
    def _():
        for h in range(9):
            direct(h).wait_send()

    @pl.when(far)
    def _():
        for h in range(9):
            (direct if VIA[h] is None else hop)(h).wait_send()

    for via in (0, 1):

        @pl.when(carries(via))
        def _():
            for h in range(9):
                if VIA[h] == via:
                    onward(h).wait_send()


def store(*refs):
    sems = refs[10]
    copies = [pltpu.make_async_copy(refs[i], refs[5 + i], sems.at[i]) for i in range(5)]
    for copy in copies:
        copy.start()
    for copy in copies:
        copy.wait()


def shards(features, weight_x, weight_y, conv_weight, class_bias):
    vmem = pl.BlockSpec(memory_space=pltpu.VMEM)
    hbm = pl.BlockSpec(memory_space=pltpu.HBM)
    dma = pltpu.SemaphoreType.DMA
    shapes = (
        jax.ShapeDtypeStruct((6, 256, 512), BF16),
        jax.ShapeDtypeStruct((6, 128, 128), BF16),
        jax.ShapeDtypeStruct((384, 32), BF16),
        jax.ShapeDtypeStruct((192, 64), BF16),
        jax.ShapeDtypeStruct((48, 32), BF16),
    )
    outs = pl.pallas_call(
        kernel,
        name="blend",
        out_shape=shapes,
        in_specs=[hbm] * 5,
        out_specs=(vmem,) * 5,
        scratch_shapes=[
            pltpu.SMEM((56,), jnp.int32),
            pltpu.SMEM((40,), jnp.int32),
            pltpu.VMEM((32, 32), BF16),
            pltpu.VMEM((1, 32), F32),
            pltpu.VMEM((7, 256, 640), BF16),
            pltpu.VMEM((256, 256), BF16),
            pltpu.VMEM((6, 256, 128), BF16),
            pltpu.VMEM((6, 256, 128), BF16),
            pltpu.VMEM((272, 128), BF16),
            pltpu.VMEM((272, 128), BF16),
            pltpu.VMEM((4, 256, 128), BF16),
            pltpu.VMEM((4, 256, 128), BF16),
            pltpu.VMEM((32, 128), BF16),
            pltpu.VMEM((32, 128), BF16),
            pltpu.VMEM((5, 128, 128), BF16),
            pltpu.VMEM((256, 128), F32),
            pltpu.VMEM((2, 8, 128), F32),
            pltpu.VMEM((512, 128), BF16),
            pltpu.VMEM((128, 128), BF16),
            pltpu.VMEM((128, 128), BF16),
            pltpu.VMEM((128, 128), BF16),
            pltpu.VMEM((512, 128), BF16),
            pltpu.VMEM((16, 128), BF16),
            pltpu.VMEM((8, 16, 128), BF16),
            dma((11,)),
            dma((7,)),
            dma((7,)),
            dma((9,)),
            dma((9,)),
            dma((5,)),
            dma((5,)),
            dma((5,)),
            dma((8,)),
            dma((8,)),
            pltpu.SemaphoreType.REGULAR((4,)),
        ],
        compiler_params=pltpu.CompilerParams(
            collective_id=0, has_side_effects=True, vmem_limit_bytes=24 << 20
        ),
    )(
        *(
            pltpu.with_memory_space_constraint(value, pltpu.HBM)
            for value in (
                features.reshape(7, 256, 640),
                weight_x,
                weight_y,
                conv_weight,
                class_bias.reshape(1, 32),
            )
        )
    )
    outs = pl.pallas_call(
        store,
        name="store",
        out_shape=shapes,
        in_specs=[pl.BlockSpec(memory_space=pl.ANY)] * 5,
        out_specs=(hbm,) * 5,
        scratch_shapes=[dma((5,))],
        compiler_params=pltpu.CompilerParams(vmem_limit_bytes=1 << 20),
    )(*outs)
    return (
        outs[0].reshape(48, 32, 512),
        outs[1].reshape(24, 32, 128),
        outs[2].reshape(12, 32, 32),
        outs[3].reshape(6, 32, 64),
        outs[4].reshape(3, 16, 32).transpose(0, 2, 1),
    )


def solution(mesh):
    placed = (P("gx", None, "gy"), P("gx"), P("gy"), P(), P())
    return jax.shard_map(
        shards,
        mesh=mesh,
        in_specs=placed,
        out_specs=(
            P("gx", None, "gy"),
            P("gx", None, "gy"),
            P("gx", None, "gy"),
            P("gx", None, None),
            P("gx", None, None),
        ),
        check_vma=False,
    )
```

```python
import jax
import jax.numpy as jnp
from jax import lax
from jax.experimental import pallas as pl
from jax.experimental.pallas import tpu as pltpu
from jax.sharding import PartitionSpec as P

MESH = pl.DeviceIdType.MESH
F32 = jnp.float32
BF16 = jnp.bfloat16

CHUNKS = 6
ROWS = 256
PIECES = ((1, 0), (1, 1), (2, 0), (2, 1), (3, 0), (3, 1), (0, 0), (0, 1))
POOLED = 8
VIA = (0, 0, 1, 1, 2, 2, None, None, None)


def iota(shape, dim):
    return lax.broadcasted_iota(jnp.int32, shape, dim)


def one_hot(condition, value):
    return jnp.where(condition, value, 0.0).astype(BF16)


def dot(a, b):
    return jnp.dot(a, b, preferred_element_type=F32)


def device(x, y, z, core):
    return (z * 8 + (y // 4) * 4 + x, (y % 4) * 2 + core)


def kernel(
    features,
    weight_x_in,
    weight_y_in,
    conv_in,
    bias_in,
    out0,
    out1,
    level2,
    level3,
    level4,
    weight_x,
    weight_y,
    conv,
    bias,
    held,
    block,
    y_out,
    y_in,
    corner_out,
    corner_in,
    x_out,
    x_in,
    pooled_out,
    pooled_in,
    relay,
    first_y,
    shares,
    pool1,
    pool2,
    pool3,
    pool4,
    pool_row,
    own_third,
    all_third,
    own_first,
    all_first,
    load_sem,
    y_send,
    y_recv,
    x_send,
    x_recv,
    hop_send,
    hop_recv,
    on_send,
    third_send,
    third_recv,
    told,
):
    gx = lax.axis_index("gx")
    gy = lax.axis_index("gy")
    x, z, core = gx % 4, gx // 8, gy % 2
    y = (gx // 4) % 2 * 4 + gy // 2
    near = x < 3
    far = jnp.logical_and(x == 3, gx < 63)
    has_left = gx > 0
    has_up = gy > 0
    has_down = gy < 7
    far_in = jnp.logical_and(x == 0, has_left)
    passing = jnp.logical_not(jnp.logical_and(z == 7, y >= 4))

    def carries(via):
        return jnp.logical_and(x == via, passing)

    names = (
        (conv_in, conv),
        (bias_in, bias),
        (weight_x_in, weight_x),
        (weight_y_in, weight_y),
    )
    loads = [
        pltpu.make_async_copy(features.at[i], held.at[i], load_sem.at[i])
        for i in range(7)
    ]
    small = [
        pltpu.make_async_copy(src, dst, load_sem.at[7 + i])
        for i, (src, dst) in enumerate(names)
    ]
    small[0].start()
    loads[6].start()
    for copy in small[1:]:
        copy.start()
    for i in range(CHUNKS):
        loads[i].start()

    barrier = pltpu.get_barrier_semaphore()

    def tell(semaphore, target):
        pl.semaphore_signal(semaphore, inc=1, device_id=target, device_id_type=MESH)

    middle = jnp.logical_and(x == 2, passing)

    for via in (0, 1, 2):

        @pl.when(carries(via))
        def _():
            tell(barrier, device(3, y, z, core))
            if via != 2:
                tell(barrier, device(2, y, z, core))

    @pl.when(far)
    def _():
        tell(barrier, device(2, y, z, core))

    @pl.when(far_in)
    def _():
        before = z - jnp.where(y < 4, 1, 0)
        tell(barrier, device(2, (y + 4) % 8, before, core))

    @pl.when(x > 0)
    def _():
        tell(barrier, (gx - 1, gy))

    def tell_group(semaphore, steps):
        @pl.when(gy >= steps)
        def _():
            tell(semaphore, (gx, gy - steps))

        @pl.when(gy + steps < 8)
        def _():
            tell(semaphore, (gx, gy + steps))

    def in_group(steps):
        return (gy >= steps).astype(jnp.int32) + (gy + steps < 8).astype(jnp.int32)

    tell_group(barrier, 1)

    for copy in small:
        copy.wait()

    table = jnp.concatenate(
        [conv[...].astype(F32), jnp.broadcast_to(bias[...], (8, 32))], axis=0
    )
    table = jnp.concatenate([table, jnp.zeros((40, 96), F32)], axis=1).T[:32]
    wide = jnp.concatenate([table[:, :32]] * 4, axis=1)
    tall = jnp.concatenate([wide] * 8, axis=0)
    for t in range(2):
        columns = iota((ROWS, 128), 1) + 128 * t
        same = iota((ROWS, 128), 0) // 32 == columns // 32
        block[:, 128 * t : 128 * (t + 1)] = jnp.where(same, tall, 0.0).astype(BF16)
    bias_column = jnp.concatenate([table[:, 32:33]] * 8, axis=0)

    def logits(i, lanes):
        return (dot(block[...], held[i, :, lanes]) + bias_column).astype(BF16)

    lane_y = iota((8, 128), 1) // 16
    row = iota((8, 128), 0)
    nothing = jnp.zeros((8, 128), F32)
    wy_own, wy_last, wx_own, wx_last, wx_own_lane, wx_last_lane = (nothing,) * 6
    for k in range(8):
        own, last = weight_y[k].astype(F32), weight_y[32 + k].astype(F32)
        wy_own = jnp.where(lane_y == k, own, wy_own)
        wy_last = jnp.where(lane_y == k, last, wy_last)
        own, last = weight_x[k].astype(F32), weight_x[48 + k].astype(F32)
        wx_own = jnp.where(row == k, own, wx_own)
        wx_last = jnp.where(row == k, last, wx_last)
        wx_own_lane = jnp.where(lane_y == k, own, wx_own_lane)
        wx_last_lane = jnp.where(lane_y == k, last, wx_last_lane)
    corner_out[ROWS:, :] = jnp.concatenate([wy_last, wy_last], axis=0).astype(BF16)
    pooled_out[16:, :] = jnp.concatenate([wx_last, wx_last_lane], axis=0).astype(BF16)

    loads[6].wait()
    corner_out[:ROWS, :] = logits(6, slice(512, 640))

    peers = in_group(1) + near.astype(jnp.int32)
    peers = peers + 3 * far.astype(jnp.int32) + 4 * middle.astype(jnp.int32)
    pl.semaphore_wait(barrier, peers)

    @pl.when(middle)
    def _():
        for source_x in (3, 0, 1):
            tell(told.at[0], device(source_x, y, z, core))

    tell_group(told.at[1], 1)

    def remote(src, dst, send, recv, target):
        return pltpu.make_async_remote_copy(
            src_ref=src,
            dst_ref=dst,
            send_sem=send,
            recv_sem=recv,
            device_id=target,
            device_id_type=MESH,
        )

    down = (gx, (gy + 1) % 8)
    corner_copy = remote(corner_out, corner_in, y_send.at[6], y_recv.at[6], down)
    y_copies = [
        remote(y_out.at[i], y_in.at[i], y_send.at[i], y_recv.at[i], down)
        for i in range(CHUNKS)
    ]

    def part(ref, h):
        t, half = PIECES[h]
        return ref.at[t, pl.ds(128 * half, 128)]

    def direct(h):
        target = ((gx + 1) % 64, gy)
        if h == POOLED:
            src, dst = pooled_out, pooled_in
        else:
            src, dst = part(x_out, h), part(x_in, h)
        return remote(src, dst, x_send.at[h], x_recv.at[h], target)

    def hop(h):
        target = device(VIA[h], y, z, core)
        return remote(
            part(x_out, h), relay.at[h], hop_send.at[h], hop_recv.at[h], target
        )

    def onward(h):
        target = device(0, (y + 4) % 8, z + y // 4, core)
        return remote(
            relay.at[h], part(x_in, h), on_send.at[h], x_recv.at[h], target
        )

    def send_x(pieces):
        @pl.when(near)
        def _():
            for h in pieces:
                direct(h).start()

        @pl.when(far)
        def _():
            for h in pieces:
                (direct if VIA[h] is None else hop)(h).start()

    @pl.when(has_down)
    def _():
        corner_copy.start()

    margin = logits(6, slice(0, 512))
    for t in range(4):
        x_out[t] = margin[:, 128 * t : 128 * (t + 1)]

    send_x((0, 1, 2, 3, 4, 5))

    for i in (1, 2, 3, 4, 5, 0):
        loads[i].wait()
        y_out[i] = logits(i, slice(512, 640))

        @pl.when(has_down)
        def _():
            y_copies[i].start()

    for i in range(CHUNKS):
        out0[i] = logits(i, slice(0, 512))

    pl.semaphore_wait(told.at[1], in_group(1))
    tell_group(told.at[2], 2)

    source, target = iota((512, 128), 0), iota((512, 128), 1)
    pool1[...] = one_hot(source // 32 * 8 + source % 16 // 2 == target, 0.125)
    pool_row[...] = one_hot(
        source // 128 * 2 + source % 16 // 8 == target % 8, 1.0 / 512
    )
    source, target = iota((128, 128), 0), iota((128, 128), 1)
    pool2[...] = one_hot(source // 16 * 4 + source % 8 // 2 == target, 0.125)
    pool4[...] = one_hot(jnp.logical_and(source // 4 == target, source < 64), 0.125)
    pool3[...] = one_hot(
        jnp.logical_and(source // 8 * 2 + source % 4 // 2 == target % 8, source < 32),
        0.125,
    )

    @pl.when(far)
    def _():
        pl.semaphore_wait(told.at[0], 1)


    for via in (0, 1, 2):

        @pl.when(carries(via))
        def _():
            if via != 2:
                pl.semaphore_wait(told.at[0], 1)
            for h in range(9):
                if VIA[h] == via:
                    hop(h).wait_recv()
                    onward(h).start()

    def pool_rows(tiles):
        return sum(dot(v, pool_row[128 * t : 128 * (t + 1)]) for t, v in tiles)

    group = iota((16, 128), 1) // 8
    rows = pool_rows([(t, x_out[t]) for t in range(1, 4)])

    @pl.when(has_up)
    def _():
        corner_copy.wait_recv()
        wy_up = corner_in[ROWS:, :].astype(F32)[:8]
        total = wy_own + wy_up
        own_share, up_share = wy_own / total, wy_up / total
        shares[0] = own_share
        shares[1] = up_share
        x_out[0] = (
            x_out[0].astype(F32) * own_share[:1]
            + corner_in[:ROWS, :].astype(F32) * up_share[:1]
        ).astype(BF16)

    rows = rows + pool_rows([(0, x_out[0])])
    value = jnp.zeros((16, 128), F32)
    for g in range(16):
        value = jnp.where(group == g, rows[16 * g : 16 * (g + 1)], value)
    pooled_out[:16, :] = value.astype(BF16)
    send_x((POOLED, 6, 7))

    pl.semaphore_wait(told.at[2], in_group(2))
    tell_group(told.at[3], 4)

    third = jnp.zeros((16, 128), F32)

    def place(third, i, value):
        third = jnp.where(group == (gy + i) % 16, value[:16], third)
        return jnp.where(group == (gy + 6 + i) % 16, value[16:], third)

    def mips(i, pooled):
        pooled = pooled.reshape(4, 2, 32, 128)
        first = (pooled[:, 0] + pooled[:, 1]).astype(BF16).reshape(128, 128)
        out1[i] = first
        pooled = dot(first, pool2[...]).reshape(2, 2, 32, 128)
        second = (pooled[:, 0] + pooled[:, 1]).astype(BF16).reshape(64, 128)
        level2[pl.ds(64 * i, 64), :] = second[:, :32]
        return second

    for i in range(1, CHUNKS):

        @pl.when(has_up)
        def _():
            y_copies[i].wait_recv()
            out0[i, :, :128] = (
                out0[i, :, :128].astype(F32) * shares[0, :1]
                + y_in[i].astype(F32) * shares[1, :1]
            ).astype(BF16)

        pooled = dot(mips(i, dot(out0[i], pool1[...])), pool3[...])
        third = place(third, i, pooled[:32] + pooled[32:])

    def gather(own, everyone, first_sem):
        copies = [
            remote(
                own,
                everyone.at[o],
                third_send.at[first_sem + o],
                third_recv.at[first_sem + o],
                (gx, (gy + o) % 8),
            )
            for o in range(1, 8)
        ]
        for copy in copies:
            copy.start()
        return copies

    def blocks(own, everyone):
        return [own[...].astype(F32)] + [everyone[o].astype(F32) for o in range(1, 8)]

    pl.semaphore_wait(told.at[3], 1)
    own_third[...] = third.astype(BF16)
    third_copies = gather(own_third, all_third, 0)

    first_y[...] = out0[0, :, :128].astype(F32)

    @pl.when(has_up)
    def _():
        y_copies[0].wait_recv()
        first_y[...] = first_y[...] * shares[0, :1] + y_in[0].astype(F32) * shares[1, :1]

    rows = pool_rows(
        [(0, first_y[...].astype(BF16))]
        + [(t, out0[0, :, 128 * t : 128 * (t + 1)]) for t in range(1, 4)]
    )

    @pl.when(has_left)
    def _():
        direct(POOLED).wait_recv()

    @pl.when(jnp.logical_not(has_left))
    def _():
        pooled_in[...] = jnp.zeros((32, 128), BF16)

    left = pooled_in[...].astype(F32)
    wx_left, wx_left_lane = left[16:24], left[24:]
    own_share = wx_own / (wx_own + wx_left)
    left_share = wx_left / (wx_own + wx_left)
    value = jnp.zeros((32, 128), F32)
    for a in range(8):
        value = value + rows[32 * a : 32 * (a + 1)] * own_share[a : a + 1]
    other = left[:16] * (wx_left_lane / (wx_own_lane + wx_left_lane))[:1]
    for shift in (64, 32, 16):
        other = other + pltpu.roll(other, shift, 1)
    turned = pltpu.roll(other, 8, 1)
    even = group % 2 == 0
    value = value + jnp.concatenate(
        [jnp.where(even, other, turned), jnp.where(even, turned, other)], axis=0
    )
    own_first[...] = jnp.where(group < 8, value[:16], value[16:]).astype(BF16)
    first_copies = gather(own_first, all_first, 8)

    pooled = jnp.zeros((ROWS, 128), F32)
    for t in (1, 2, 3, 0):
        lanes = slice(128 * t, 128 * (t + 1))
        if t == 0:
            for copy in third_copies:
                copy.wait_recv()
            parts = blocks(own_third, all_third)
            rows = []
            for q in (1, 7, 2, 8, 3, 9, 4, 10, 5, 11):
                owner = (group - q + 16) % 16
                value = jnp.zeros((16, 128), F32)
                for o in range(8):
                    value = jnp.where(owner == (gy - o + 8) % 8, parts[o], value)
                rows.append(pltpu.roll(value, 128 - 8 * q, 1))
            later = jnp.concatenate(rows, axis=0).astype(BF16)
            level3[32:, :] = later[:, :64]
            fourth = dot(later[32:], pool4[...]).reshape(2, 2, 32, 128)
            fourth = fourth[:, 0] + fourth[:, 1]
            for i in range(2):
                level4[16 * i + 16 : 16 * i + 32, :] = fourth[i].T[:16].astype(BF16)

            @pl.when(jnp.logical_not(has_left))
            def _():
                out0[0, :, :128] = first_y[...].astype(BF16)

        @pl.when(has_left)
        def _():
            for h in range(8):
                if PIECES[h][0] == t:
                    direct(h).wait_recv()
            for a in range(8):
                part_rows = slice(32 * a, 32 * (a + 1))
                if t == 0:
                    own = first_y[part_rows, :]
                else:
                    own = out0[0, part_rows, lanes].astype(F32)
                out0[0, part_rows, lanes] = (
                    own * own_share[a : a + 1]
                    + x_in[t, part_rows, :].astype(F32) * left_share[a : a + 1]
                ).astype(BF16)

        pooled = pooled + dot(out0[0, :, lanes], pool1[lanes, :])

    mips(0, pooled)

    for copy in first_copies:
        copy.wait_recv()
    parts = blocks(own_first, all_first)
    value = jnp.zeros((16, 128), F32)
    for o in range(8):
        value = jnp.where(group % 8 == (gy - o + 8) % 8, parts[o], value)
    value = jnp.concatenate([value, pltpu.roll(value, 64, 1)], axis=0).astype(BF16)
    level3[:32, :] = value[:, :64]
    fourth = dot(value, pool4[...]) + dot(later[:32], pool4[...])
    level4[:16, :] = fourth.T[:16].astype(BF16)

    for copy in third_copies + first_copies:
        copy.wait_send()

    @pl.when(has_down)
    def _():
        corner_copy.wait_send()
        for i in range(CHUNKS):
            y_copies[i].wait_send()

    @pl.when(near)
    def _():
        for h in range(9):
            direct(h).wait_send()

    @pl.when(far)
    def _():
        for h in range(9):
            (direct if VIA[h] is None else hop)(h).wait_send()

    for via in (0, 1, 2):

        @pl.when(carries(via))
        def _():
            for h in range(9):
                if VIA[h] == via:
                    onward(h).wait_send()


def store(*refs):
    sems = refs[10]
    copies = [pltpu.make_async_copy(refs[i], refs[5 + i], sems.at[i]) for i in range(5)]
    for copy in copies:
        copy.start()
    for copy in copies:
        copy.wait()


def shards(features, weight_x, weight_y, conv_weight, class_bias):
    vmem = pl.BlockSpec(memory_space=pltpu.VMEM)
    hbm = pl.BlockSpec(memory_space=pltpu.HBM)
    dma = pltpu.SemaphoreType.DMA
    shapes = (
        jax.ShapeDtypeStruct((6, 256, 512), BF16),
        jax.ShapeDtypeStruct((6, 128, 128), BF16),
        jax.ShapeDtypeStruct((384, 32), BF16),
        jax.ShapeDtypeStruct((192, 64), BF16),
        jax.ShapeDtypeStruct((48, 32), BF16),
    )
    outs = pl.pallas_call(
        kernel,
        name="blend",
        out_shape=shapes,
        in_specs=[hbm] * 5,
        out_specs=(vmem,) * 5,
        scratch_shapes=[
            pltpu.SMEM((56,), jnp.int32),
            pltpu.SMEM((40,), jnp.int32),
            pltpu.VMEM((32, 32), BF16),
            pltpu.VMEM((1, 32), F32),
            pltpu.VMEM((7, 256, 640), BF16),
            pltpu.VMEM((256, 256), BF16),
            pltpu.VMEM((6, 256, 128), BF16),
            pltpu.VMEM((6, 256, 128), BF16),
            pltpu.VMEM((272, 128), BF16),
            pltpu.VMEM((272, 128), BF16),
            pltpu.VMEM((4, 256, 128), BF16),
            pltpu.VMEM((4, 256, 128), BF16),
            pltpu.VMEM((32, 128), BF16),
            pltpu.VMEM((32, 128), BF16),
            pltpu.VMEM((6, 128, 128), BF16),
            pltpu.VMEM((256, 128), F32),
            pltpu.VMEM((2, 8, 128), F32),
            pltpu.VMEM((512, 128), BF16),
            pltpu.VMEM((128, 128), BF16),
            pltpu.VMEM((128, 128), BF16),
            pltpu.VMEM((128, 128), BF16),
            pltpu.VMEM((512, 128), BF16),
            pltpu.VMEM((16, 128), BF16),
            pltpu.VMEM((8, 16, 128), BF16),
            pltpu.VMEM((16, 128), BF16),
            pltpu.VMEM((8, 16, 128), BF16),
            dma((11,)),
            dma((7,)),
            dma((7,)),
            dma((9,)),
            dma((9,)),
            dma((6,)),
            dma((6,)),
            dma((6,)),
            dma((16,)),
            dma((16,)),
            pltpu.SemaphoreType.REGULAR((4,)),
        ],
        compiler_params=pltpu.CompilerParams(
            collective_id=0, has_side_effects=True, vmem_limit_bytes=24 << 20
        ),
    )(
        *(
            pltpu.with_memory_space_constraint(value, pltpu.HBM)
            for value in (
                features.reshape(7, 256, 640),
                weight_x,
                weight_y,
                conv_weight,
                class_bias.reshape(1, 32),
            )
        )
    )
    outs = pl.pallas_call(
        store,
        name="store",
        out_shape=shapes,
        in_specs=[pl.BlockSpec(memory_space=pl.ANY)] * 5,
        out_specs=(hbm,) * 5,
        scratch_shapes=[dma((5,))],
        compiler_params=pltpu.CompilerParams(vmem_limit_bytes=1 << 20),
    )(*outs)
    return (
        outs[0].reshape(48, 32, 512),
        outs[1].reshape(24, 32, 128),
        outs[2].reshape(12, 32, 32),
        outs[3].reshape(6, 32, 64),
        outs[4].reshape(3, 16, 32).transpose(0, 2, 1),
    )


def solution(mesh):
    placed = (P("gx", None, "gy"), P("gx"), P("gy"), P(), P())
    return jax.shard_map(
        shards,
        mesh=mesh,
        in_specs=placed,
        out_specs=(
            P("gx", None, "gy"),
            P("gx", None, "gy"),
            P("gx", None, "gy"),
            P("gx", None, None),
            P("gx", None, None),
        ),
        check_vma=False,
    )
```

```python
import jax
import jax.numpy as jnp
from jax import lax
from jax.experimental import pallas as pl
from jax.experimental.pallas import tpu as pltpu
from jax.sharding import PartitionSpec as P

MESH = pl.DeviceIdType.MESH
F32 = jnp.float32
BF16 = jnp.bfloat16

CHUNKS = 6
ROWS = 256
PIECES = ((1, 0), (1, 1), (2, 0), (2, 1), (3, 0), (3, 1), (0, 0), (0, 1))
POOLED = 8
VIA = (0, 0, 1, 1, 1, 2, None, None, None)


def iota(shape, dim):
    return lax.broadcasted_iota(jnp.int32, shape, dim)


def one_hot(condition, value):
    return jnp.where(condition, value, 0.0).astype(BF16)


def dot(a, b):
    return jnp.dot(a, b, preferred_element_type=F32)


def device(x, y, z, core):
    return (z * 8 + (y // 4) * 4 + x, (y % 4) * 2 + core)


def kernel(
    features,
    weight_x_in,
    weight_y_in,
    conv_in,
    bias_in,
    out0,
    out1,
    level2,
    level3,
    level4,
    weight_x,
    weight_y,
    conv,
    bias,
    held,
    block,
    y_out,
    y_in,
    corner_out,
    corner_in,
    x_out,
    x_in,
    pooled_out,
    pooled_in,
    relay,
    first_y,
    shares,
    pool1,
    pool2,
    pool3,
    pool4,
    pool_row,
    own_third,
    all_third,
    own_first,
    all_first,
    load_sem,
    y_send,
    y_recv,
    x_send,
    x_recv,
    hop_send,
    hop_recv,
    on_send,
    third_send,
    third_recv,
    told,
):
    gx = lax.axis_index("gx")
    gy = lax.axis_index("gy")
    x, z, core = gx % 4, gx // 8, gy % 2
    y = (gx // 4) % 2 * 4 + gy // 2
    near = x < 3
    far = jnp.logical_and(x == 3, gx < 63)
    has_left = gx > 0
    has_up = gy > 0
    has_down = gy < 7
    far_in = jnp.logical_and(x == 0, has_left)
    passing = jnp.logical_not(jnp.logical_and(z == 7, y >= 4))

    def carries(via):
        return jnp.logical_and(x == via, passing)

    names = (
        (conv_in, conv),
        (bias_in, bias),
        (weight_x_in, weight_x),
        (weight_y_in, weight_y),
    )
    loads = [
        pltpu.make_async_copy(features.at[i], held.at[i], load_sem.at[i])
        for i in range(7)
    ]
    small = [
        pltpu.make_async_copy(src, dst, load_sem.at[7 + i])
        for i, (src, dst) in enumerate(names)
    ]
    small[0].start()
    loads[6].start()
    for copy in small[1:]:
        copy.start()
    for i in range(CHUNKS):
        loads[i].start()

    barrier = pltpu.get_barrier_semaphore()

    def tell(semaphore, target):
        pl.semaphore_signal(semaphore, inc=1, device_id=target, device_id_type=MESH)

    middle = jnp.logical_and(x == 2, passing)

    for via in (0, 1, 2):

        @pl.when(carries(via))
        def _():
            tell(barrier, device(3, y, z, core))
            if via != 2:
                tell(barrier, device(2, y, z, core))

    @pl.when(far)
    def _():
        tell(barrier, device(2, y, z, core))

    @pl.when(far_in)
    def _():
        before = z - jnp.where(y < 4, 1, 0)
        tell(barrier, device(2, (y + 4) % 8, before, core))

    @pl.when(x > 0)
    def _():
        tell(barrier, (gx - 1, gy))

    def tell_group(semaphore, steps):
        @pl.when(gy >= steps)
        def _():
            tell(semaphore, (gx, gy - steps))

        @pl.when(gy + steps < 8)
        def _():
            tell(semaphore, (gx, gy + steps))

    def in_group(steps):
        return (gy >= steps).astype(jnp.int32) + (gy + steps < 8).astype(jnp.int32)

    tell_group(barrier, 1)

    for copy in small:
        copy.wait()

    table = jnp.concatenate(
        [conv[...].astype(F32), jnp.broadcast_to(bias[...], (8, 32))], axis=0
    )
    table = jnp.concatenate([table, jnp.zeros((40, 96), F32)], axis=1).T[:32]
    wide = jnp.concatenate([table[:, :32]] * 4, axis=1)
    tall = jnp.concatenate([wide] * 8, axis=0)
    for t in range(2):
        columns = iota((ROWS, 128), 1) + 128 * t
        same = iota((ROWS, 128), 0) // 32 == columns // 32
        block[:, 128 * t : 128 * (t + 1)] = jnp.where(same, tall, 0.0).astype(BF16)
    bias_column = jnp.concatenate([table[:, 32:33]] * 8, axis=0)

    def logits(i, lanes):
        return (dot(block[...], held[i, :, lanes]) + bias_column).astype(BF16)

    lane_y = iota((8, 128), 1) // 16
    row = iota((8, 128), 0)
    nothing = jnp.zeros((8, 128), F32)
    wy_own, wy_last, wx_own, wx_last, wx_own_lane, wx_last_lane = (nothing,) * 6
    for k in range(8):
        own, last = weight_y[k].astype(F32), weight_y[32 + k].astype(F32)
        wy_own = jnp.where(lane_y == k, own, wy_own)
        wy_last = jnp.where(lane_y == k, last, wy_last)
        own, last = weight_x[k].astype(F32), weight_x[48 + k].astype(F32)
        wx_own = jnp.where(row == k, own, wx_own)
        wx_last = jnp.where(row == k, last, wx_last)
        wx_own_lane = jnp.where(lane_y == k, own, wx_own_lane)
        wx_last_lane = jnp.where(lane_y == k, last, wx_last_lane)
    corner_out[ROWS:, :] = jnp.concatenate([wy_last, wy_last], axis=0).astype(BF16)
    pooled_out[16:, :] = jnp.concatenate([wx_last, wx_last_lane], axis=0).astype(BF16)

    loads[6].wait()
    corner_out[:ROWS, :] = logits(6, slice(512, 640))

    peers = in_group(1) + near.astype(jnp.int32)
    peers = peers + 3 * far.astype(jnp.int32) + 4 * middle.astype(jnp.int32)
    pl.semaphore_wait(barrier, peers)

    @pl.when(middle)
    def _():
        for source_x in (3, 0, 1):
            tell(told.at[0], device(source_x, y, z, core))

    tell_group(told.at[1], 1)

    def remote(src, dst, send, recv, target):
        return pltpu.make_async_remote_copy(
            src_ref=src,
            dst_ref=dst,
            send_sem=send,
            recv_sem=recv,
            device_id=target,
            device_id_type=MESH,
        )

    down = (gx, (gy + 1) % 8)
    corner_copy = remote(corner_out, corner_in, y_send.at[6], y_recv.at[6], down)
    y_copies = [
        remote(y_out.at[i], y_in.at[i], y_send.at[i], y_recv.at[i], down)
        for i in range(CHUNKS)
    ]

    def part(ref, h):
        t, half = PIECES[h]
        return ref.at[t, pl.ds(128 * half, 128)]

    def direct(h):
        target = ((gx + 1) % 64, gy)
        if h == POOLED:
            src, dst = pooled_out, pooled_in
        else:
            src, dst = part(x_out, h), part(x_in, h)
        return remote(src, dst, x_send.at[h], x_recv.at[h], target)

    def hop(h):
        target = device(VIA[h], y, z, core)
        return remote(
            part(x_out, h), relay.at[h], hop_send.at[h], hop_recv.at[h], target
        )

    def onward(h):
        target = device(0, (y + 4) % 8, z + y // 4, core)
        return remote(
            relay.at[h], part(x_in, h), on_send.at[h], x_recv.at[h], target
        )

    def send_x(pieces):
        @pl.when(near)
        def _():
            for h in pieces:
                direct(h).start()

        @pl.when(far)
        def _():
            for h in pieces:
                (direct if VIA[h] is None else hop)(h).start()

    @pl.when(has_down)
    def _():
        corner_copy.start()

    margin = logits(6, slice(0, 512))
    for t in range(4):
        x_out[t] = margin[:, 128 * t : 128 * (t + 1)]

    send_x((0, 1, 2, 3, 4, 5))

    for i in (1, 2, 3, 4, 5, 0):
        loads[i].wait()
        y_out[i] = logits(i, slice(512, 640))

        @pl.when(has_down)
        def _():
            y_copies[i].start()

    for i in range(CHUNKS):
        out0[i] = logits(i, slice(0, 512))

    pl.semaphore_wait(told.at[1], in_group(1))
    tell_group(told.at[2], 2)

    source, target = iota((512, 128), 0), iota((512, 128), 1)
    pool1[...] = one_hot(source // 32 * 8 + source % 16 // 2 == target, 0.125)
    pool_row[...] = one_hot(
        source // 128 * 2 + source % 16 // 8 == target % 8, 1.0 / 512
    )
    source, target = iota((128, 128), 0), iota((128, 128), 1)
    pool2[...] = one_hot(source // 16 * 4 + source % 8 // 2 == target, 0.125)
    pool4[...] = one_hot(jnp.logical_and(source // 4 == target, source < 64), 0.125)
    pool3[...] = one_hot(
        jnp.logical_and(source // 8 * 2 + source % 4 // 2 == target % 8, source < 32),
        0.125,
    )

    @pl.when(far)
    def _():
        pl.semaphore_wait(told.at[0], 1)


    for via in (0, 1, 2):

        @pl.when(carries(via))
        def _():
            if via != 2:
                pl.semaphore_wait(told.at[0], 1)
            for h in range(9):
                if VIA[h] == via:
                    hop(h).wait_recv()
                    onward(h).start()

    def pool_rows(tiles):
        return sum(dot(v, pool_row[128 * t : 128 * (t + 1)]) for t, v in tiles)

    group = iota((16, 128), 1) // 8
    rows = pool_rows([(t, x_out[t]) for t in range(1, 4)])

    @pl.when(has_up)
    def _():
        corner_copy.wait_recv()
        wy_up = corner_in[ROWS:, :].astype(F32)[:8]
        total = wy_own + wy_up
        own_share, up_share = wy_own / total, wy_up / total
        shares[0] = own_share
        shares[1] = up_share
        x_out[0] = (
            x_out[0].astype(F32) * own_share[:1]
            + corner_in[:ROWS, :].astype(F32) * up_share[:1]
        ).astype(BF16)

    rows = rows + pool_rows([(0, x_out[0])])
    value = jnp.zeros((16, 128), F32)
    for g in range(16):
        value = jnp.where(group == g, rows[16 * g : 16 * (g + 1)], value)
    pooled_out[:16, :] = value.astype(BF16)
    send_x((POOLED, 6, 7))

    pl.semaphore_wait(told.at[2], in_group(2))
    tell_group(told.at[3], 4)

    third = jnp.zeros((16, 128), F32)

    def place(third, i, value):
        third = jnp.where(group == (gy + i) % 16, value[:16], third)
        return jnp.where(group == (gy + 6 + i) % 16, value[16:], third)

    def mips(i, pooled):
        pooled = pooled.reshape(4, 2, 32, 128)
        first = (pooled[:, 0] + pooled[:, 1]).astype(BF16).reshape(128, 128)
        out1[i] = first
        pooled = dot(first, pool2[...]).reshape(2, 2, 32, 128)
        second = (pooled[:, 0] + pooled[:, 1]).astype(BF16).reshape(64, 128)
        level2[pl.ds(64 * i, 64), :] = second[:, :32]
        return second

    for i in range(1, CHUNKS):

        @pl.when(has_up)
        def _():
            y_copies[i].wait_recv()
            out0[i, :, :128] = (
                out0[i, :, :128].astype(F32) * shares[0, :1]
                + y_in[i].astype(F32) * shares[1, :1]
            ).astype(BF16)

        pooled = dot(mips(i, dot(out0[i], pool1[...])), pool3[...])
        third = place(third, i, pooled[:32] + pooled[32:])

    def gather(own, everyone, first_sem):
        copies = [
            remote(
                own,
                everyone.at[o],
                third_send.at[first_sem + o],
                third_recv.at[first_sem + o],
                (gx, (gy + o) % 8),
            )
            for o in range(1, 8)
        ]
        for copy in copies:
            copy.start()
        return copies

    def blocks(own, everyone):
        return [own[...].astype(F32)] + [everyone[o].astype(F32) for o in range(1, 8)]

    pl.semaphore_wait(told.at[3], 1)
    own_third[...] = third.astype(BF16)
    third_copies = gather(own_third, all_third, 0)

    first_y[...] = out0[0, :, :128].astype(F32)

    @pl.when(has_up)
    def _():
        y_copies[0].wait_recv()
        first_y[...] = first_y[...] * shares[0, :1] + y_in[0].astype(F32) * shares[1, :1]

    rows = pool_rows(
        [(0, first_y[...].astype(BF16))]
        + [(t, out0[0, :, 128 * t : 128 * (t + 1)]) for t in range(1, 4)]
    )

    @pl.when(has_left)
    def _():
        direct(POOLED).wait_recv()

    @pl.when(jnp.logical_not(has_left))
    def _():
        pooled_in[...] = jnp.zeros((32, 128), BF16)

    left = pooled_in[...].astype(F32)
    wx_left, wx_left_lane = left[16:24], left[24:]
    own_share = wx_own / (wx_own + wx_left)
    left_share = wx_left / (wx_own + wx_left)
    value = jnp.zeros((32, 128), F32)
    for a in range(8):
        value = value + rows[32 * a : 32 * (a + 1)] * own_share[a : a + 1]
    other = left[:16] * (wx_left_lane / (wx_own_lane + wx_left_lane))[:1]
    for shift in (64, 32, 16):
        other = other + pltpu.roll(other, shift, 1)
    turned = pltpu.roll(other, 8, 1)
    even = group % 2 == 0
    value = value + jnp.concatenate(
        [jnp.where(even, other, turned), jnp.where(even, turned, other)], axis=0
    )
    own_first[...] = jnp.where(group < 8, value[:16], value[16:]).astype(BF16)
    first_copies = gather(own_first, all_first, 8)

    pooled = jnp.zeros((ROWS, 128), F32)
    for t in (1, 2, 3, 0):
        lanes = slice(128 * t, 128 * (t + 1))
        if t == 0:
            for copy in third_copies:
                copy.wait_recv()
            parts = blocks(own_third, all_third)
            rows = []
            for q in (1, 7, 2, 8, 3, 9, 4, 10, 5, 11):
                owner = (group - q + 16) % 16
                value = jnp.zeros((16, 128), F32)
                for o in range(8):
                    value = jnp.where(owner == (gy - o + 8) % 8, parts[o], value)
                rows.append(pltpu.roll(value, 128 - 8 * q, 1))
            later = jnp.concatenate(rows, axis=0).astype(BF16)
            level3[32:, :] = later[:, :64]
            fourth = dot(later[32:], pool4[...]).reshape(2, 2, 32, 128)
            fourth = fourth[:, 0] + fourth[:, 1]
            for i in range(2):
                level4[16 * i + 16 : 16 * i + 32, :] = fourth[i].T[:16].astype(BF16)

            @pl.when(jnp.logical_not(has_left))
            def _():
                out0[0, :, :128] = first_y[...].astype(BF16)

        @pl.when(has_left)
        def _():
            for h in range(8):
                if PIECES[h][0] == t:
                    direct(h).wait_recv()
            for a in range(8):
                part_rows = slice(32 * a, 32 * (a + 1))
                if t == 0:
                    own = first_y[part_rows, :]
                else:
                    own = out0[0, part_rows, lanes].astype(F32)
                out0[0, part_rows, lanes] = (
                    own * own_share[a : a + 1]
                    + x_in[t, part_rows, :].astype(F32) * left_share[a : a + 1]
                ).astype(BF16)

        pooled = pooled + dot(out0[0, :, lanes], pool1[lanes, :])

    mips(0, pooled)

    for copy in first_copies:
        copy.wait_recv()
    parts = blocks(own_first, all_first)
    value = jnp.zeros((16, 128), F32)
    for o in range(8):
        value = jnp.where(group % 8 == (gy - o + 8) % 8, parts[o], value)
    value = jnp.concatenate([value, pltpu.roll(value, 64, 1)], axis=0).astype(BF16)
    level3[:32, :] = value[:, :64]
    fourth = dot(value, pool4[...]) + dot(later[:32], pool4[...])
    level4[:16, :] = fourth.T[:16].astype(BF16)

    for copy in third_copies + first_copies:
        copy.wait_send()

    @pl.when(has_down)
    def _():
        corner_copy.wait_send()
        for i in range(CHUNKS):
            y_copies[i].wait_send()

    @pl.when(near)
    def _():
        for h in range(9):
            direct(h).wait_send()

    @pl.when(far)
    def _():
        for h in range(9):
            (direct if VIA[h] is None else hop)(h).wait_send()

    for via in (0, 1, 2):

        @pl.when(carries(via))
        def _():
            for h in range(9):
                if VIA[h] == via:
                    onward(h).wait_send()


def store(*refs):
    sems = refs[10]
    copies = [pltpu.make_async_copy(refs[i], refs[5 + i], sems.at[i]) for i in range(5)]
    for copy in copies:
        copy.start()
    for copy in copies:
        copy.wait()


def shards(features, weight_x, weight_y, conv_weight, class_bias):
    vmem = pl.BlockSpec(memory_space=pltpu.VMEM)
    hbm = pl.BlockSpec(memory_space=pltpu.HBM)
    dma = pltpu.SemaphoreType.DMA
    shapes = (
        jax.ShapeDtypeStruct((6, 256, 512), BF16),
        jax.ShapeDtypeStruct((6, 128, 128), BF16),
        jax.ShapeDtypeStruct((384, 32), BF16),
        jax.ShapeDtypeStruct((192, 64), BF16),
        jax.ShapeDtypeStruct((48, 32), BF16),
    )
    outs = pl.pallas_call(
        kernel,
        name="blend",
        out_shape=shapes,
        in_specs=[hbm] * 5,
        out_specs=(vmem,) * 5,
        scratch_shapes=[
            pltpu.SMEM((56,), jnp.int32),
            pltpu.SMEM((40,), jnp.int32),
            pltpu.VMEM((32, 32), BF16),
            pltpu.VMEM((1, 32), F32),
            pltpu.VMEM((7, 256, 640), BF16),
            pltpu.VMEM((256, 256), BF16),
            pltpu.VMEM((6, 256, 128), BF16),
            pltpu.VMEM((6, 256, 128), BF16),
            pltpu.VMEM((272, 128), BF16),
            pltpu.VMEM((272, 128), BF16),
            pltpu.VMEM((4, 256, 128), BF16),
            pltpu.VMEM((4, 256, 128), BF16),
            pltpu.VMEM((32, 128), BF16),
            pltpu.VMEM((32, 128), BF16),
            pltpu.VMEM((6, 128, 128), BF16),
            pltpu.VMEM((256, 128), F32),
            pltpu.VMEM((2, 8, 128), F32),
            pltpu.VMEM((512, 128), BF16),
            pltpu.VMEM((128, 128), BF16),
            pltpu.VMEM((128, 128), BF16),
            pltpu.VMEM((128, 128), BF16),
            pltpu.VMEM((512, 128), BF16),
            pltpu.VMEM((16, 128), BF16),
            pltpu.VMEM((8, 16, 128), BF16),
            pltpu.VMEM((16, 128), BF16),
            pltpu.VMEM((8, 16, 128), BF16),
            dma((11,)),
            dma((7,)),
            dma((7,)),
            dma((9,)),
            dma((9,)),
            dma((6,)),
            dma((6,)),
            dma((6,)),
            dma((16,)),
            dma((16,)),
            pltpu.SemaphoreType.REGULAR((4,)),
        ],
        compiler_params=pltpu.CompilerParams(
            collective_id=0, has_side_effects=True, vmem_limit_bytes=24 << 20
        ),
    )(
        *(
            pltpu.with_memory_space_constraint(value, pltpu.HBM)
            for value in (
                features.reshape(7, 256, 640),
                weight_x,
                weight_y,
                conv_weight,
                class_bias.reshape(1, 32),
            )
        )
    )
    outs = pl.pallas_call(
        store,
        name="store",
        out_shape=shapes,
        in_specs=[pl.BlockSpec(memory_space=pl.ANY)] * 5,
        out_specs=(hbm,) * 5,
        scratch_shapes=[dma((5,))],
        compiler_params=pltpu.CompilerParams(vmem_limit_bytes=1 << 20),
    )(*outs)
    return (
        outs[0].reshape(48, 32, 512),
        outs[1].reshape(24, 32, 128),
        outs[2].reshape(12, 32, 32),
        outs[3].reshape(6, 32, 64),
        outs[4].reshape(3, 16, 32).transpose(0, 2, 1),
    )


def solution(mesh):
    placed = (P("gx", None, "gy"), P("gx"), P("gy"), P(), P())
    return jax.shard_map(
        shards,
        mesh=mesh,
        in_specs=placed,
        out_specs=(
            P("gx", None, "gy"),
            P("gx", None, "gy"),
            P("gx", None, "gy"),
            P("gx", None, None),
            P("gx", None, None),
        ),
        check_vma=False,
    )
```

```python
import jax
import jax.numpy as jnp
from jax import lax
from jax.experimental import pallas as pl
from jax.experimental.pallas import tpu as pltpu
from jax.sharding import PartitionSpec as P

MESH = pl.DeviceIdType.MESH
F32 = jnp.float32
BF16 = jnp.bfloat16

CHUNKS = 6
ROWS = 256
PIECES = ((1, 0), (1, 1), (2, 0), (2, 1), (3, 0), (3, 1), (0, 0), (0, 1))
POOLED = 8
VIA = (2, 1, 1, 1, 0, 0, None, None, None)


def iota(shape, dim):
    return lax.broadcasted_iota(jnp.int32, shape, dim)


def one_hot(condition, value):
    return jnp.where(condition, value, 0.0).astype(BF16)


def dot(a, b):
    return jnp.dot(a, b, preferred_element_type=F32)


def device(x, y, z, core):
    return (z * 8 + (y // 4) * 4 + x, (y % 4) * 2 + core)


def kernel(
    features,
    weight_x_in,
    weight_y_in,
    conv_in,
    bias_in,
    out0,
    out1,
    level2,
    level3,
    level4,
    weight_x,
    weight_y,
    conv,
    bias,
    held,
    block,
    y_out,
    y_in,
    corner_out,
    corner_in,
    x_out,
    x_in,
    pooled_out,
    pooled_in,
    relay,
    first_y,
    shares,
    pool1,
    pool2,
    pool3,
    pool4,
    pool_row,
    own_third,
    all_third,
    own_first,
    all_first,
    load_sem,
    y_send,
    y_recv,
    x_send,
    x_recv,
    hop_send,
    hop_recv,
    on_send,
    third_send,
    third_recv,
    told,
):
    gx = lax.axis_index("gx")
    gy = lax.axis_index("gy")
    x, z, core = gx % 4, gx // 8, gy % 2
    y = (gx // 4) % 2 * 4 + gy // 2
    near = x < 3
    far = jnp.logical_and(x == 3, gx < 63)
    has_left = gx > 0
    has_up = gy > 0
    has_down = gy < 7
    far_in = jnp.logical_and(x == 0, has_left)
    passing = jnp.logical_not(jnp.logical_and(z == 7, y >= 4))

    def carries(via):
        return jnp.logical_and(x == via, passing)

    names = (
        (conv_in, conv),
        (bias_in, bias),
        (weight_x_in, weight_x),
        (weight_y_in, weight_y),
    )
    loads = [
        pltpu.make_async_copy(features.at[i], held.at[i], load_sem.at[i])
        for i in range(7)
    ]
    small = [
        pltpu.make_async_copy(src, dst, load_sem.at[7 + i])
        for i, (src, dst) in enumerate(names)
    ]
    small[0].start()
    loads[6].start()
    for copy in small[1:]:
        copy.start()
    for i in range(CHUNKS):
        loads[i].start()

    barrier = pltpu.get_barrier_semaphore()

    def tell(semaphore, target):
        pl.semaphore_signal(semaphore, inc=1, device_id=target, device_id_type=MESH)

    middle = jnp.logical_and(x == 2, passing)

    for via in (0, 1, 2):

        @pl.when(carries(via))
        def _():
            tell(barrier, device(3, y, z, core))
            if via != 2:
                tell(barrier, device(2, y, z, core))

    @pl.when(far)
    def _():
        tell(barrier, device(2, y, z, core))

    @pl.when(far_in)
    def _():
        before = z - jnp.where(y < 4, 1, 0)
        tell(barrier, device(2, (y + 4) % 8, before, core))

    @pl.when(x > 0)
    def _():
        tell(barrier, (gx - 1, gy))

    def tell_group(semaphore, steps):
        @pl.when(gy >= steps)
        def _():
            tell(semaphore, (gx, gy - steps))

        @pl.when(gy + steps < 8)
        def _():
            tell(semaphore, (gx, gy + steps))

    def in_group(steps):
        return (gy >= steps).astype(jnp.int32) + (gy + steps < 8).astype(jnp.int32)

    tell_group(barrier, 1)

    for copy in small:
        copy.wait()

    table = jnp.concatenate(
        [conv[...].astype(F32), jnp.broadcast_to(bias[...], (8, 32))], axis=0
    )
    table = jnp.concatenate([table, jnp.zeros((40, 96), F32)], axis=1).T[:32]
    wide = jnp.concatenate([table[:, :32]] * 4, axis=1)
    tall = jnp.concatenate([wide] * 8, axis=0)
    for t in range(2):
        columns = iota((ROWS, 128), 1) + 128 * t
        same = iota((ROWS, 128), 0) // 32 == columns // 32
        block[:, 128 * t : 128 * (t + 1)] = jnp.where(same, tall, 0.0).astype(BF16)
    bias_column = jnp.concatenate([table[:, 32:33]] * 8, axis=0)

    def logits(i, lanes):
        return (dot(block[...], held[i, :, lanes]) + bias_column).astype(BF16)

    lane_y = iota((8, 128), 1) // 16
    row = iota((8, 128), 0)
    nothing = jnp.zeros((8, 128), F32)
    wy_own, wy_last, wx_own, wx_last, wx_own_lane, wx_last_lane = (nothing,) * 6
    for k in range(8):
        own, last = weight_y[k].astype(F32), weight_y[32 + k].astype(F32)
        wy_own = jnp.where(lane_y == k, own, wy_own)
        wy_last = jnp.where(lane_y == k, last, wy_last)
        own, last = weight_x[k].astype(F32), weight_x[48 + k].astype(F32)
        wx_own = jnp.where(row == k, own, wx_own)
        wx_last = jnp.where(row == k, last, wx_last)
        wx_own_lane = jnp.where(lane_y == k, own, wx_own_lane)
        wx_last_lane = jnp.where(lane_y == k, last, wx_last_lane)
    corner_out[ROWS:, :] = jnp.concatenate([wy_last, wy_last], axis=0).astype(BF16)
    pooled_out[16:, :] = jnp.concatenate([wx_last, wx_last_lane], axis=0).astype(BF16)

    loads[6].wait()
    corner_out[:ROWS, :] = logits(6, slice(512, 640))

    peers = in_group(1) + near.astype(jnp.int32)
    peers = peers + 3 * far.astype(jnp.int32) + 4 * middle.astype(jnp.int32)
    pl.semaphore_wait(barrier, peers)

    @pl.when(middle)
    def _():
        for source_x in (3, 0, 1):
            tell(told.at[0], device(source_x, y, z, core))

    tell_group(told.at[1], 1)

    def remote(src, dst, send, recv, target):
        return pltpu.make_async_remote_copy(
            src_ref=src,
            dst_ref=dst,
            send_sem=send,
            recv_sem=recv,
            device_id=target,
            device_id_type=MESH,
        )

    down = (gx, (gy + 1) % 8)
    corner_copy = remote(corner_out, corner_in, y_send.at[6], y_recv.at[6], down)
    y_copies = [
        remote(y_out.at[i], y_in.at[i], y_send.at[i], y_recv.at[i], down)
        for i in range(CHUNKS)
    ]

    def part(ref, h):
        t, half = PIECES[h]
        return ref.at[t, pl.ds(128 * half, 128)]

    def direct(h):
        target = ((gx + 1) % 64, gy)
        if h == POOLED:
            src, dst = pooled_out, pooled_in
        else:
            src, dst = part(x_out, h), part(x_in, h)
        return remote(src, dst, x_send.at[h], x_recv.at[h], target)

    def hop(h):
        target = device(VIA[h], y, z, core)
        return remote(
            part(x_out, h), relay.at[h], hop_send.at[h], hop_recv.at[h], target
        )

    def onward(h):
        target = device(0, (y + 4) % 8, z + y // 4, core)
        return remote(
            relay.at[h], part(x_in, h), on_send.at[h], x_recv.at[h], target
        )

    def send_x(pieces):
        @pl.when(near)
        def _():
            for h in pieces:
                direct(h).start()

        @pl.when(far)
        def _():
            for h in pieces:
                (direct if VIA[h] is None else hop)(h).start()

    @pl.when(has_down)
    def _():
        corner_copy.start()

    margin = logits(6, slice(0, 512))
    for t in range(4):
        x_out[t] = margin[:, 128 * t : 128 * (t + 1)]

    send_x((0, 1, 2, 3, 4, 5))

    not_far = jnp.logical_not(far)
    for i in (1, 2, 3, 4, 5, 0):
        loads[i].wait()
        y_out[i] = logits(i, slice(512, 640))

        @pl.when(jnp.logical_and(has_down, jnp.logical_or(not_far, i in (1, 2, 3, 4))))
        def _():
            y_copies[i].start()

    for i in range(CHUNKS):
        out0[i] = logits(i, slice(0, 512))

    pl.semaphore_wait(told.at[1], in_group(1))
    tell_group(told.at[2], 2)

    source, target = iota((512, 128), 0), iota((512, 128), 1)
    pool1[...] = one_hot(source // 32 * 8 + source % 16 // 2 == target, 0.125)
    pool_row[...] = one_hot(
        source // 128 * 2 + source % 16 // 8 == target % 8, 1.0 / 512
    )
    source, target = iota((128, 128), 0), iota((128, 128), 1)
    pool2[...] = one_hot(source // 16 * 4 + source % 8 // 2 == target, 0.125)
    pool4[...] = one_hot(jnp.logical_and(source // 4 == target, source < 64), 0.125)
    pool3[...] = one_hot(
        jnp.logical_and(source // 8 * 2 + source % 4 // 2 == target % 8, source < 32),
        0.125,
    )

    @pl.when(far)
    def _():
        pl.semaphore_wait(told.at[0], 1)


    for via in (0, 1, 2):

        @pl.when(carries(via))
        def _():
            if via != 2:
                pl.semaphore_wait(told.at[0], 1)
            for h in range(9):
                if VIA[h] == via:
                    hop(h).wait_recv()
                    onward(h).start()

    def pool_rows(tiles):
        return sum(dot(v, pool_row[128 * t : 128 * (t + 1)]) for t, v in tiles)

    group = iota((16, 128), 1) // 8
    rows = pool_rows([(t, x_out[t]) for t in range(1, 4)])

    @pl.when(has_up)
    def _():
        corner_copy.wait_recv()
        wy_up = corner_in[ROWS:, :].astype(F32)[:8]
        total = wy_own + wy_up
        own_share, up_share = wy_own / total, wy_up / total
        shares[0] = own_share
        shares[1] = up_share
        x_out[0] = (
            x_out[0].astype(F32) * own_share[:1]
            + corner_in[:ROWS, :].astype(F32) * up_share[:1]
        ).astype(BF16)

    rows = rows + pool_rows([(0, x_out[0])])
    value = jnp.zeros((16, 128), F32)
    for g in range(16):
        value = jnp.where(group == g, rows[16 * g : 16 * (g + 1)], value)
    pooled_out[:16, :] = value.astype(BF16)
    send_x((POOLED, 6, 7))

    @pl.when(jnp.logical_and(has_down, far))
    def _():
        for i in (5, 0):
            y_copies[i].start()

    pl.semaphore_wait(told.at[2], in_group(2))
    tell_group(told.at[3], 4)

    third = jnp.zeros((16, 128), F32)

    def place(third, i, value):
        third = jnp.where(group == (gy + i) % 16, value[:16], third)
        return jnp.where(group == (gy + 6 + i) % 16, value[16:], third)

    def mips(i, pooled):
        pooled = pooled.reshape(4, 2, 32, 128)
        first = (pooled[:, 0] + pooled[:, 1]).astype(BF16).reshape(128, 128)
        out1[i] = first
        pooled = dot(first, pool2[...]).reshape(2, 2, 32, 128)
        second = (pooled[:, 0] + pooled[:, 1]).astype(BF16).reshape(64, 128)
        level2[pl.ds(64 * i, 64), :] = second[:, :32]
        return second

    for i in range(1, CHUNKS):

        @pl.when(has_up)
        def _():
            y_copies[i].wait_recv()
            out0[i, :, :128] = (
                out0[i, :, :128].astype(F32) * shares[0, :1]
                + y_in[i].astype(F32) * shares[1, :1]
            ).astype(BF16)

        pooled = dot(mips(i, dot(out0[i], pool1[...])), pool3[...])
        third = place(third, i, pooled[:32] + pooled[32:])

    def gather(own, everyone, first_sem):
        copies = [
            remote(
                own,
                everyone.at[o],
                third_send.at[first_sem + o],
                third_recv.at[first_sem + o],
                (gx, (gy + o) % 8),
            )
            for o in range(1, 8)
        ]
        for copy in copies:
            copy.start()
        return copies

    def blocks(own, everyone):
        return [own[...].astype(F32)] + [everyone[o].astype(F32) for o in range(1, 8)]

    pl.semaphore_wait(told.at[3], 1)
    own_third[...] = third.astype(BF16)
    third_copies = gather(own_third, all_third, 0)

    first_y[...] = out0[0, :, :128].astype(F32)

    @pl.when(has_up)
    def _():
        y_copies[0].wait_recv()
        first_y[...] = first_y[...] * shares[0, :1] + y_in[0].astype(F32) * shares[1, :1]

    rows = pool_rows(
        [(0, first_y[...].astype(BF16))]
        + [(t, out0[0, :, 128 * t : 128 * (t + 1)]) for t in range(1, 4)]
    )

    @pl.when(has_left)
    def _():
        direct(POOLED).wait_recv()

    @pl.when(jnp.logical_not(has_left))
    def _():
        pooled_in[...] = jnp.zeros((32, 128), BF16)

    left = pooled_in[...].astype(F32)
    wx_left, wx_left_lane = left[16:24], left[24:]
    own_share = wx_own / (wx_own + wx_left)
    left_share = wx_left / (wx_own + wx_left)
    value = jnp.zeros((32, 128), F32)
    for a in range(8):
        value = value + rows[32 * a : 32 * (a + 1)] * own_share[a : a + 1]
    other = left[:16] * (wx_left_lane / (wx_own_lane + wx_left_lane))[:1]
    for shift in (64, 32, 16):
        other = other + pltpu.roll(other, shift, 1)
    turned = pltpu.roll(other, 8, 1)
    even = group % 2 == 0
    value = value + jnp.concatenate(
        [jnp.where(even, other, turned), jnp.where(even, turned, other)], axis=0
    )
    own_first[...] = jnp.where(group < 8, value[:16], value[16:]).astype(BF16)
    first_copies = gather(own_first, all_first, 8)

    pooled = jnp.zeros((ROWS, 128), F32)
    for t in (1, 2, 3, 0):
        lanes = slice(128 * t, 128 * (t + 1))
        if t == 0:
            for copy in third_copies:
                copy.wait_recv()
            parts = blocks(own_third, all_third)
            rows = []
            for q in (1, 7, 2, 8, 3, 9, 4, 10, 5, 11):
                owner = (group - q + 16) % 16
                value = jnp.zeros((16, 128), F32)
                for o in range(8):
                    value = jnp.where(owner == (gy - o + 8) % 8, parts[o], value)
                rows.append(pltpu.roll(value, 128 - 8 * q, 1))
            later = jnp.concatenate(rows, axis=0).astype(BF16)
            level3[32:, :] = later[:, :64]
            fourth = dot(later[32:], pool4[...]).reshape(2, 2, 32, 128)
            fourth = fourth[:, 0] + fourth[:, 1]
            for i in range(2):
                level4[16 * i + 16 : 16 * i + 32, :] = fourth[i].T[:16].astype(BF16)

            @pl.when(jnp.logical_not(has_left))
            def _():
                out0[0, :, :128] = first_y[...].astype(BF16)

        @pl.when(has_left)
        def _():
            for h in range(8):
                if PIECES[h][0] == t:
                    direct(h).wait_recv()
            for a in range(8):
                part_rows = slice(32 * a, 32 * (a + 1))
                if t == 0:
                    own = first_y[part_rows, :]
                else:
                    own = out0[0, part_rows, lanes].astype(F32)
                out0[0, part_rows, lanes] = (
                    own * own_share[a : a + 1]
                    + x_in[t, part_rows, :].astype(F32) * left_share[a : a + 1]
                ).astype(BF16)

        pooled = pooled + dot(out0[0, :, lanes], pool1[lanes, :])

    mips(0, pooled)

    for copy in first_copies:
        copy.wait_recv()
    parts = blocks(own_first, all_first)
    value = jnp.zeros((16, 128), F32)
    for o in range(8):
        value = jnp.where(group % 8 == (gy - o + 8) % 8, parts[o], value)
    value = jnp.concatenate([value, pltpu.roll(value, 64, 1)], axis=0).astype(BF16)
    level3[:32, :] = value[:, :64]
    fourth = dot(value, pool4[...]) + dot(later[:32], pool4[...])
    level4[:16, :] = fourth.T[:16].astype(BF16)

    for copy in third_copies + first_copies:
        copy.wait_send()

    @pl.when(has_down)
    def _():
        corner_copy.wait_send()
        for i in range(CHUNKS):
            y_copies[i].wait_send()

    @pl.when(near)
    def _():
        for h in range(9):
            direct(h).wait_send()

    @pl.when(far)
    def _():
        for h in range(9):
            (direct if VIA[h] is None else hop)(h).wait_send()

    for via in (0, 1, 2):

        @pl.when(carries(via))
        def _():
            for h in range(9):
                if VIA[h] == via:
                    onward(h).wait_send()


def store(*refs):
    sems = refs[10]
    copies = [pltpu.make_async_copy(refs[i], refs[5 + i], sems.at[i]) for i in range(5)]
    for copy in copies:
        copy.start()
    for copy in copies:
        copy.wait()


def shards(features, weight_x, weight_y, conv_weight, class_bias):
    vmem = pl.BlockSpec(memory_space=pltpu.VMEM)
    hbm = pl.BlockSpec(memory_space=pltpu.HBM)
    dma = pltpu.SemaphoreType.DMA
    shapes = (
        jax.ShapeDtypeStruct((6, 256, 512), BF16),
        jax.ShapeDtypeStruct((6, 128, 128), BF16),
        jax.ShapeDtypeStruct((384, 32), BF16),
        jax.ShapeDtypeStruct((192, 64), BF16),
        jax.ShapeDtypeStruct((48, 32), BF16),
    )
    outs = pl.pallas_call(
        kernel,
        name="blend",
        out_shape=shapes,
        in_specs=[hbm] * 5,
        out_specs=(vmem,) * 5,
        scratch_shapes=[
            pltpu.SMEM((56,), jnp.int32),
            pltpu.SMEM((40,), jnp.int32),
            pltpu.VMEM((32, 32), BF16),
            pltpu.VMEM((1, 32), F32),
            pltpu.VMEM((7, 256, 640), BF16),
            pltpu.VMEM((256, 256), BF16),
            pltpu.VMEM((6, 256, 128), BF16),
            pltpu.VMEM((6, 256, 128), BF16),
            pltpu.VMEM((272, 128), BF16),
            pltpu.VMEM((272, 128), BF16),
            pltpu.VMEM((4, 256, 128), BF16),
            pltpu.VMEM((4, 256, 128), BF16),
            pltpu.VMEM((32, 128), BF16),
            pltpu.VMEM((32, 128), BF16),
            pltpu.VMEM((6, 128, 128), BF16),
            pltpu.VMEM((256, 128), F32),
            pltpu.VMEM((2, 8, 128), F32),
            pltpu.VMEM((512, 128), BF16),
            pltpu.VMEM((128, 128), BF16),
            pltpu.VMEM((128, 128), BF16),
            pltpu.VMEM((128, 128), BF16),
            pltpu.VMEM((512, 128), BF16),
            pltpu.VMEM((16, 128), BF16),
            pltpu.VMEM((8, 16, 128), BF16),
            pltpu.VMEM((16, 128), BF16),
            pltpu.VMEM((8, 16, 128), BF16),
            dma((11,)),
            dma((7,)),
            dma((7,)),
            dma((9,)),
            dma((9,)),
            dma((6,)),
            dma((6,)),
            dma((6,)),
            dma((16,)),
            dma((16,)),
            pltpu.SemaphoreType.REGULAR((4,)),
        ],
        compiler_params=pltpu.CompilerParams(
            collective_id=0, has_side_effects=True, vmem_limit_bytes=24 << 20
        ),
    )(
        *(
            pltpu.with_memory_space_constraint(value, pltpu.HBM)
            for value in (
                features.reshape(7, 256, 640),
                weight_x,
                weight_y,
                conv_weight,
                class_bias.reshape(1, 32),
            )
        )
    )
    outs = pl.pallas_call(
        store,
        name="store",
        out_shape=shapes,
        in_specs=[pl.BlockSpec(memory_space=pl.ANY)] * 5,
        out_specs=(hbm,) * 5,
        scratch_shapes=[dma((5,))],
        compiler_params=pltpu.CompilerParams(vmem_limit_bytes=1 << 20),
    )(*outs)
    return (
        outs[0].reshape(48, 32, 512),
        outs[1].reshape(24, 32, 128),
        outs[2].reshape(12, 32, 32),
        outs[3].reshape(6, 32, 64),
        outs[4].reshape(3, 16, 32).transpose(0, 2, 1),
    )


def solution(mesh):
    placed = (P("gx", None, "gy"), P("gx"), P("gy"), P(), P())
    return jax.shard_map(
        shards,
        mesh=mesh,
        in_specs=placed,
        out_specs=(
            P("gx", None, "gy"),
            P("gx", None, "gy"),
            P("gx", None, "gy"),
            P("gx", None, None),
            P("gx", None, None),
        ),
        check_vma=False,
    )
```

```python
import jax
import jax.numpy as jnp
from jax import lax
from jax.experimental import pallas as pl
from jax.experimental.pallas import tpu as pltpu
from jax.sharding import PartitionSpec as P

MESH = pl.DeviceIdType.MESH
F32 = jnp.float32
BF16 = jnp.bfloat16

CHUNKS = 6
ROWS = 256
PIECES = ((1, 0), (1, 1), (2, 0), (2, 1), (3, 0), (3, 1), (0, 0), (0, 1))
POOLED = 8
VIA = (1, 1, 0, 0, 2, 1, None, None, None)


def iota(shape, dim):
    return lax.broadcasted_iota(jnp.int32, shape, dim)


def one_hot(condition, value):
    return jnp.where(condition, value, 0.0).astype(BF16)


def dot(a, b):
    return jnp.dot(a, b, preferred_element_type=F32)


def device(x, y, z, core):
    return (z * 8 + (y // 4) * 4 + x, (y % 4) * 2 + core)


def kernel(
    features,
    weight_x_in,
    weight_y_in,
    conv_in,
    bias_in,
    out0,
    out1,
    level2,
    level3,
    level4,
    weight_x,
    weight_y,
    conv,
    bias,
    held,
    block,
    y_out,
    y_in,
    corner_out,
    corner_in,
    x_out,
    x_in,
    pooled_out,
    pooled_in,
    relay,
    first_y,
    shares,
    pool1,
    pool2,
    pool3,
    pool4,
    pool_row,
    own_third,
    all_third,
    own_first,
    all_first,
    load_sem,
    y_send,
    y_recv,
    x_send,
    x_recv,
    hop_send,
    hop_recv,
    on_send,
    third_send,
    third_recv,
    told,
):
    gx = lax.axis_index("gx")
    gy = lax.axis_index("gy")
    x, z, core = gx % 4, gx // 8, gy % 2
    y = (gx // 4) % 2 * 4 + gy // 2
    near = x < 3
    far = jnp.logical_and(x == 3, gx < 63)
    has_left = gx > 0
    has_up = gy > 0
    has_down = gy < 7
    far_in = jnp.logical_and(x == 0, has_left)
    passing = jnp.logical_not(jnp.logical_and(z == 7, y >= 4))

    def carries(via):
        return jnp.logical_and(x == via, passing)

    names = (
        (conv_in, conv),
        (bias_in, bias),
        (weight_x_in, weight_x),
        (weight_y_in, weight_y),
    )
    loads = [
        pltpu.make_async_copy(features.at[i], held.at[i], load_sem.at[i])
        for i in range(7)
    ]
    small = [
        pltpu.make_async_copy(src, dst, load_sem.at[7 + i])
        for i, (src, dst) in enumerate(names)
    ]
    small[0].start()
    loads[6].start()
    for copy in small[1:]:
        copy.start()
    for i in range(CHUNKS):
        loads[i].start()

    barrier = pltpu.get_barrier_semaphore()

    def tell(semaphore, target):
        pl.semaphore_signal(semaphore, inc=1, device_id=target, device_id_type=MESH)

    middle = jnp.logical_and(x == 2, passing)

    for via in (0, 1, 2):

        @pl.when(carries(via))
        def _():
            tell(barrier, device(3, y, z, core))
            if via != 2:
                tell(barrier, device(2, y, z, core))

    @pl.when(far)
    def _():
        tell(barrier, device(2, y, z, core))

    @pl.when(far_in)
    def _():
        before = z - jnp.where(y < 4, 1, 0)
        tell(barrier, device(2, (y + 4) % 8, before, core))

    @pl.when(x > 0)
    def _():
        tell(barrier, (gx - 1, gy))

    def tell_group(semaphore, steps):
        @pl.when(gy >= steps)
        def _():
            tell(semaphore, (gx, gy - steps))

        @pl.when(gy + steps < 8)
        def _():
            tell(semaphore, (gx, gy + steps))

    def in_group(steps):
        return (gy >= steps).astype(jnp.int32) + (gy + steps < 8).astype(jnp.int32)

    tell_group(barrier, 1)

    for copy in small:
        copy.wait()

    table = jnp.concatenate(
        [conv[...].astype(F32), jnp.broadcast_to(bias[...], (8, 32))], axis=0
    )
    table = jnp.concatenate([table, jnp.zeros((40, 96), F32)], axis=1).T[:32]
    wide = jnp.concatenate([table[:, :32]] * 4, axis=1)
    tall = jnp.concatenate([wide] * 8, axis=0)
    for t in range(2):
        columns = iota((ROWS, 128), 1) + 128 * t
        same = iota((ROWS, 128), 0) // 32 == columns // 32
        block[:, 128 * t : 128 * (t + 1)] = jnp.where(same, tall, 0.0).astype(BF16)
    bias_column = jnp.concatenate([table[:, 32:33]] * 8, axis=0)

    def logits(i, lanes):
        return (dot(block[...], held[i, :, lanes]) + bias_column).astype(BF16)

    lane_y = iota((8, 128), 1) // 16
    row = iota((8, 128), 0)
    nothing = jnp.zeros((8, 128), F32)
    wy_own, wy_last, wx_own, wx_last, wx_own_lane, wx_last_lane = (nothing,) * 6
    for k in range(8):
        own, last = weight_y[k].astype(F32), weight_y[32 + k].astype(F32)
        wy_own = jnp.where(lane_y == k, own, wy_own)
        wy_last = jnp.where(lane_y == k, last, wy_last)
        own, last = weight_x[k].astype(F32), weight_x[48 + k].astype(F32)
        wx_own = jnp.where(row == k, own, wx_own)
        wx_last = jnp.where(row == k, last, wx_last)
        wx_own_lane = jnp.where(lane_y == k, own, wx_own_lane)
        wx_last_lane = jnp.where(lane_y == k, last, wx_last_lane)
    corner_out[ROWS:, :] = jnp.concatenate([wy_last, wy_last], axis=0).astype(BF16)
    pooled_out[16:, :] = jnp.concatenate([wx_last, wx_last_lane], axis=0).astype(BF16)

    loads[6].wait()
    corner_out[:ROWS, :] = logits(6, slice(512, 640))

    peers = in_group(1) + near.astype(jnp.int32)
    peers = peers + 3 * far.astype(jnp.int32) + 4 * middle.astype(jnp.int32)
    pl.semaphore_wait(barrier, peers)

    @pl.when(middle)
    def _():
        for source_x in (3, 0, 1):
            tell(told.at[0], device(source_x, y, z, core))

    tell_group(told.at[1], 1)

    def remote(src, dst, send, recv, target):
        return pltpu.make_async_remote_copy(
            src_ref=src,
            dst_ref=dst,
            send_sem=send,
            recv_sem=recv,
            device_id=target,
            device_id_type=MESH,
        )

    down = (gx, (gy + 1) % 8)
    corner_copy = remote(corner_out, corner_in, y_send.at[6], y_recv.at[6], down)
    y_copies = [
        remote(y_out.at[i], y_in.at[i], y_send.at[i], y_recv.at[i], down)
        for i in range(CHUNKS)
    ]

    def part(ref, h):
        t, half = PIECES[h]
        return ref.at[t, pl.ds(128 * half, 128)]

    def direct(h):
        target = ((gx + 1) % 64, gy)
        if h == POOLED:
            src, dst = pooled_out, pooled_in
        else:
            src, dst = part(x_out, h), part(x_in, h)
        return remote(src, dst, x_send.at[h], x_recv.at[h], target)

    def hop(h):
        target = device(VIA[h], y, z, core)
        return remote(
            part(x_out, h), relay.at[h], hop_send.at[h], hop_recv.at[h], target
        )

    def onward(h):
        target = device(0, (y + 4) % 8, z + y // 4, core)
        return remote(
            relay.at[h], part(x_in, h), on_send.at[h], x_recv.at[h], target
        )

    def send_x(pieces):
        @pl.when(near)
        def _():
            for h in pieces:
                direct(h).start()

        @pl.when(far)
        def _():
            for h in pieces:
                (direct if VIA[h] is None else hop)(h).start()

    @pl.when(has_down)
    def _():
        corner_copy.start()

    margin = logits(6, slice(0, 512))
    for t in range(4):
        x_out[t] = margin[:, 128 * t : 128 * (t + 1)]

    send_x((0, 1, 2, 3, 4, 5))

    not_far = jnp.logical_not(far)
    for i in (1, 2, 3, 4, 5, 0):
        loads[i].wait()
        y_out[i] = logits(i, slice(512, 640))

        @pl.when(jnp.logical_and(has_down, jnp.logical_or(not_far, i in (1, 2, 3, 4))))
        def _():
            y_copies[i].start()

    for i in range(CHUNKS):
        out0[i] = logits(i, slice(0, 512))

    pl.semaphore_wait(told.at[1], in_group(1))
    tell_group(told.at[2], 2)

    source, target = iota((512, 128), 0), iota((512, 128), 1)
    pool1[...] = one_hot(source // 32 * 8 + source % 16 // 2 == target, 0.125)
    pool_row[...] = one_hot(
        source // 128 * 2 + source % 16 // 8 == target % 8, 1.0 / 512
    )
    source, target = iota((128, 128), 0), iota((128, 128), 1)
    pool2[...] = one_hot(source // 16 * 4 + source % 8 // 2 == target, 0.125)
    pool4[...] = one_hot(jnp.logical_and(source // 4 == target, source < 64), 0.125)
    pool3[...] = one_hot(
        jnp.logical_and(source // 8 * 2 + source % 4 // 2 == target % 8, source < 32),
        0.125,
    )

    @pl.when(far)
    def _():
        pl.semaphore_wait(told.at[0], 1)


    for via in (0, 1, 2):

        @pl.when(carries(via))
        def _():
            if via != 2:
                pl.semaphore_wait(told.at[0], 1)
            for h in range(9):
                if VIA[h] == via:
                    hop(h).wait_recv()
                    onward(h).start()

    def pool_rows(tiles):
        return sum(dot(v, pool_row[128 * t : 128 * (t + 1)]) for t, v in tiles)

    group = iota((16, 128), 1) // 8
    rows = pool_rows([(t, x_out[t]) for t in range(1, 4)])

    @pl.when(has_up)
    def _():
        corner_copy.wait_recv()
        wy_up = corner_in[ROWS:, :].astype(F32)[:8]
        total = wy_own + wy_up
        own_share, up_share = wy_own / total, wy_up / total
        shares[0] = own_share
        shares[1] = up_share
        x_out[0] = (
            x_out[0].astype(F32) * own_share[:1]
            + corner_in[:ROWS, :].astype(F32) * up_share[:1]
        ).astype(BF16)

    rows = rows + pool_rows([(0, x_out[0])])
    value = jnp.zeros((16, 128), F32)
    for g in range(16):
        value = jnp.where(group == g, rows[16 * g : 16 * (g + 1)], value)
    pooled_out[:16, :] = value.astype(BF16)
    send_x((POOLED, 6, 7))

    @pl.when(jnp.logical_and(has_down, far))
    def _():
        for i in (5, 0):
            y_copies[i].start()

    pl.semaphore_wait(told.at[2], in_group(2))
    tell_group(told.at[3], 4)

    third = jnp.zeros((16, 128), F32)

    def place(third, i, value):
        third = jnp.where(group == (gy + i) % 16, value[:16], third)
        return jnp.where(group == (gy + 6 + i) % 16, value[16:], third)

    def mips(i, pooled):
        pooled = pooled.reshape(4, 2, 32, 128)
        first = (pooled[:, 0] + pooled[:, 1]).astype(BF16).reshape(128, 128)
        out1[i] = first
        pooled = dot(first, pool2[...]).reshape(2, 2, 32, 128)
        second = (pooled[:, 0] + pooled[:, 1]).astype(BF16).reshape(64, 128)
        level2[pl.ds(64 * i, 64), :] = second[:, :32]
        return second

    for i in range(1, CHUNKS):

        @pl.when(has_up)
        def _():
            y_copies[i].wait_recv()
            out0[i, :, :128] = (
                out0[i, :, :128].astype(F32) * shares[0, :1]
                + y_in[i].astype(F32) * shares[1, :1]
            ).astype(BF16)

        pooled = dot(mips(i, dot(out0[i], pool1[...])), pool3[...])
        third = place(third, i, pooled[:32] + pooled[32:])

    def gather(own, everyone, first_sem):
        copies = [
            remote(
                own,
                everyone.at[o],
                third_send.at[first_sem + o],
                third_recv.at[first_sem + o],
                (gx, (gy + o) % 8),
            )
            for o in range(1, 8)
        ]
        for copy in copies:
            copy.start()
        return copies

    def blocks(own, everyone):
        return [own[...].astype(F32)] + [everyone[o].astype(F32) for o in range(1, 8)]

    pl.semaphore_wait(told.at[3], 1)
    own_third[...] = third.astype(BF16)
    third_copies = gather(own_third, all_third, 0)

    first_y[...] = out0[0, :, :128].astype(F32)

    @pl.when(has_up)
    def _():
        y_copies[0].wait_recv()
        first_y[...] = first_y[...] * shares[0, :1] + y_in[0].astype(F32) * shares[1, :1]

    rows = pool_rows(
        [(0, first_y[...].astype(BF16))]
        + [(t, out0[0, :, 128 * t : 128 * (t + 1)]) for t in range(1, 4)]
    )

    @pl.when(has_left)
    def _():
        direct(POOLED).wait_recv()

    @pl.when(jnp.logical_not(has_left))
    def _():
        pooled_in[...] = jnp.zeros((32, 128), BF16)

    left = pooled_in[...].astype(F32)
    wx_left, wx_left_lane = left[16:24], left[24:]
    own_share = wx_own / (wx_own + wx_left)
    left_share = wx_left / (wx_own + wx_left)
    value = jnp.zeros((32, 128), F32)
    for a in range(8):
        value = value + rows[32 * a : 32 * (a + 1)] * own_share[a : a + 1]
    other = left[:16] * (wx_left_lane / (wx_own_lane + wx_left_lane))[:1]
    for shift in (64, 32, 16):
        other = other + pltpu.roll(other, shift, 1)
    turned = pltpu.roll(other, 8, 1)
    even = group % 2 == 0
    value = value + jnp.concatenate(
        [jnp.where(even, other, turned), jnp.where(even, turned, other)], axis=0
    )
    own_first[...] = jnp.where(group < 8, value[:16], value[16:]).astype(BF16)
    first_copies = gather(own_first, all_first, 8)

    pooled = jnp.zeros((ROWS, 128), F32)
    for t in (1, 2, 3, 0):
        lanes = slice(128 * t, 128 * (t + 1))
        if t == 0:
            for copy in third_copies:
                copy.wait_recv()
            parts = blocks(own_third, all_third)
            rows = []
            for q in (1, 7, 2, 8, 3, 9, 4, 10, 5, 11):
                owner = (group - q + 16) % 16
                value = jnp.zeros((16, 128), F32)
                for o in range(8):
                    value = jnp.where(owner == (gy - o + 8) % 8, parts[o], value)
                rows.append(pltpu.roll(value, 128 - 8 * q, 1))
            later = jnp.concatenate(rows, axis=0).astype(BF16)
            level3[32:, :] = later[:, :64]
            fourth = dot(later[32:], pool4[...]).reshape(2, 2, 32, 128)
            fourth = fourth[:, 0] + fourth[:, 1]
            for i in range(2):
                level4[16 * i + 16 : 16 * i + 32, :] = fourth[i].T[:16].astype(BF16)

            @pl.when(jnp.logical_not(has_left))
            def _():
                out0[0, :, :128] = first_y[...].astype(BF16)

        @pl.when(has_left)
        def _():
            for h in range(8):
                if PIECES[h][0] == t:
                    direct(h).wait_recv()
            for a in range(8):
                part_rows = slice(32 * a, 32 * (a + 1))
                if t == 0:
                    own = first_y[part_rows, :]
                else:
                    own = out0[0, part_rows, lanes].astype(F32)
                out0[0, part_rows, lanes] = (
                    own * own_share[a : a + 1]
                    + x_in[t, part_rows, :].astype(F32) * left_share[a : a + 1]
                ).astype(BF16)

        pooled = pooled + dot(out0[0, :, lanes], pool1[lanes, :])

    mips(0, pooled)

    for copy in first_copies:
        copy.wait_recv()
    parts = blocks(own_first, all_first)
    value = jnp.zeros((16, 128), F32)
    for o in range(8):
        value = jnp.where(group % 8 == (gy - o + 8) % 8, parts[o], value)
    value = jnp.concatenate([value, pltpu.roll(value, 64, 1)], axis=0).astype(BF16)
    level3[:32, :] = value[:, :64]
    fourth = dot(value, pool4[...]) + dot(later[:32], pool4[...])
    level4[:16, :] = fourth.T[:16].astype(BF16)

    for copy in third_copies + first_copies:
        copy.wait_send()

    @pl.when(has_down)
    def _():
        corner_copy.wait_send()
        for i in range(CHUNKS):
            y_copies[i].wait_send()

    @pl.when(near)
    def _():
        for h in range(9):
            direct(h).wait_send()

    @pl.when(far)
    def _():
        for h in range(9):
            (direct if VIA[h] is None else hop)(h).wait_send()

    for via in (0, 1, 2):

        @pl.when(carries(via))
        def _():
            for h in range(9):
                if VIA[h] == via:
                    onward(h).wait_send()


def store(*refs):
    sems = refs[10]
    copies = [pltpu.make_async_copy(refs[i], refs[5 + i], sems.at[i]) for i in range(5)]
    for copy in copies:
        copy.start()
    for copy in copies:
        copy.wait()


def shards(features, weight_x, weight_y, conv_weight, class_bias):
    vmem = pl.BlockSpec(memory_space=pltpu.VMEM)
    hbm = pl.BlockSpec(memory_space=pltpu.HBM)
    dma = pltpu.SemaphoreType.DMA
    shapes = (
        jax.ShapeDtypeStruct((6, 256, 512), BF16),
        jax.ShapeDtypeStruct((6, 128, 128), BF16),
        jax.ShapeDtypeStruct((384, 32), BF16),
        jax.ShapeDtypeStruct((192, 64), BF16),
        jax.ShapeDtypeStruct((48, 32), BF16),
    )
    outs = pl.pallas_call(
        kernel,
        name="blend",
        out_shape=shapes,
        in_specs=[hbm] * 5,
        out_specs=(vmem,) * 5,
        scratch_shapes=[
            pltpu.SMEM((56,), jnp.int32),
            pltpu.SMEM((40,), jnp.int32),
            pltpu.VMEM((32, 32), BF16),
            pltpu.VMEM((1, 32), F32),
            pltpu.VMEM((7, 256, 640), BF16),
            pltpu.VMEM((256, 256), BF16),
            pltpu.VMEM((6, 256, 128), BF16),
            pltpu.VMEM((6, 256, 128), BF16),
            pltpu.VMEM((272, 128), BF16),
            pltpu.VMEM((272, 128), BF16),
            pltpu.VMEM((4, 256, 128), BF16),
            pltpu.VMEM((4, 256, 128), BF16),
            pltpu.VMEM((32, 128), BF16),
            pltpu.VMEM((32, 128), BF16),
            pltpu.VMEM((6, 128, 128), BF16),
            pltpu.VMEM((256, 128), F32),
            pltpu.VMEM((2, 8, 128), F32),
            pltpu.VMEM((512, 128), BF16),
            pltpu.VMEM((128, 128), BF16),
            pltpu.VMEM((128, 128), BF16),
            pltpu.VMEM((128, 128), BF16),
            pltpu.VMEM((512, 128), BF16),
            pltpu.VMEM((16, 128), BF16),
            pltpu.VMEM((8, 16, 128), BF16),
            pltpu.VMEM((16, 128), BF16),
            pltpu.VMEM((8, 16, 128), BF16),
            dma((11,)),
            dma((7,)),
            dma((7,)),
            dma((9,)),
            dma((9,)),
            dma((6,)),
            dma((6,)),
            dma((6,)),
            dma((16,)),
            dma((16,)),
            pltpu.SemaphoreType.REGULAR((4,)),
        ],
        compiler_params=pltpu.CompilerParams(
            collective_id=0, has_side_effects=True, vmem_limit_bytes=24 << 20
        ),
    )(
        *(
            pltpu.with_memory_space_constraint(value, pltpu.HBM)
            for value in (
                features.reshape(7, 256, 640),
                weight_x,
                weight_y,
                conv_weight,
                class_bias.reshape(1, 32),
            )
        )
    )
    outs = pl.pallas_call(
        store,
        name="store",
        out_shape=shapes,
        in_specs=[pl.BlockSpec(memory_space=pl.ANY)] * 5,
        out_specs=(hbm,) * 5,
        scratch_shapes=[dma((5,))],
        compiler_params=pltpu.CompilerParams(vmem_limit_bytes=1 << 20),
    )(*outs)
    return (
        outs[0].reshape(48, 32, 512),
        outs[1].reshape(24, 32, 128),
        outs[2].reshape(12, 32, 32),
        outs[3].reshape(6, 32, 64),
        outs[4].reshape(3, 16, 32).transpose(0, 2, 1),
    )


def solution(mesh):
    placed = (P("gx", None, "gy"), P("gx"), P("gy"), P(), P())
    return jax.shard_map(
        shards,
        mesh=mesh,
        in_specs=placed,
        out_specs=(
            P("gx", None, "gy"),
            P("gx", None, "gy"),
            P("gx", None, "gy"),
            P("gx", None, None),
            P("gx", None, None),
        ),
        check_vma=False,
    )
```
